512 devices in a mesh: pair: 32 (over z_lo, y), vtile: 8 (over x, core), irrep: 2 (over z_hi).
Axes of the slice: x: 4, y: 4, z: 16 (z_hi: 2, z_lo: 8; z = z_hi * 8 + z_lo), core: 2. Of those that a mesh axis runs over, the one named last changes fastest.
Arguments:
- amplitudes: bfloat16 [160, 8, 7744], P('pair'), may hold values from -4 to 4
- slabs: bfloat16 [32, 8, 2, 88, 7744], P('pair', 'vtile', 'irrep'), may hold values from -1.5 to 1.5
- couplings: bfloat16 [2, 30, 30, 176], P(None, None, None, 'irrep'), may hold values from -6 to 6
- occ_energy: float32 [30], replicated, may hold values from -2 to -0.3
- vir_energy: float32 [8, 88], replicated, may hold values from 0.2 to 4
- occ_irrep: int32 [30], replicated, may hold values from 0 to 7
- pair_i: int32 [160], P('pair'), may hold values from 0 to 29, as said below
- pair_j: int32 [160], P('pair'), may hold values from 0 to 29, as said below
- window_k: int32 [2], replicated, may hold values from 0 to 29
- owner: int32 [2], replicated, may hold values from 0 to 31
Outputs:
- resid_part: float32 [160, 8, 7744], P('pair', 'vtile', 'irrep')
The draws below stay inside these ranges and needn't reach their ends.
Inputs may be any that keep to these rules, and one draw needn't show every extreme that they name: Pairs come in groups of 16 that share pair_i; groups have different pair_i. Within a group of pairs sharing pair_i, pair_j values are distinct.
All inputs are finite; a program needn't handle non-finite values.
Results may differ from the reference program's by a relative error of at most 0.0003.
Values may be sent and summed in bfloat16 or wider, within the bound.
A program may use at most 64 MiB of HBM per device.

```python
import jax
import jax.numpy as jnp
from jax import lax

VBLK = 88
NOCC = 30
K_WIN = 2
PAIRS = 160
SLOTS = 32
CWIN = 2


def pair_table(key):
    base_key = jax.random.fold_in(key, 7)
    first_key, second_key, slot_key = jax.random.split(base_key, 3)
    groups = PAIRS // 16
    middle_first = (jax.random.permutation(first_key, NOCC - 2)[:groups - 2] + 1).astype(jnp.int32)
    firsts = jnp.concatenate([jnp.array([0, NOCC - 1], jnp.int32), middle_first])
    group_keys = jax.random.split(second_key, groups)

    def group_seconds(member):
        middle = (jax.random.permutation(member, NOCC - 2)[:14] + 1).astype(jnp.int32)
        return jnp.concatenate([jnp.array([0, NOCC - 1], jnp.int32), middle])
    seconds = jax.vmap(group_seconds)(group_keys)
    slots = jax.random.permutation(slot_key, PAIRS)
    flat_first = jnp.repeat(firsts, 16).astype(jnp.int32)
    flat_second = seconds.reshape(-1).astype(jnp.int32)
    first_out = jnp.zeros((PAIRS,), jnp.int32).at[slots].set(flat_first)
    second_out = jnp.zeros((PAIRS,), jnp.int32).at[slots].set(flat_second)
    return (first_out, second_out)


def draw_pair_i(key, part):
    return pair_table(key)[0]


def draw_pair_j(key, part):
    return pair_table(key)[1]


def with_ends(result, key, smallest, top_value):
    dims = result.shape
    place = [jax.random.randint(jax.random.fold_in(key, axis), (), 0, dims[axis]) for axis in range(len(dims))]
    result = result.at[tuple(place)].set(smallest)
    longest = dims.index(max(dims))
    place[longest] = (place[longest] + 1) % dims[longest]
    return result.at[tuple(place)].set(top_value)


def block_scale(rng, extent, pieces, smallest, high):
    level, own = 1.0, jax.random.fold_in(rng, 6)
    for dim, parts in pieces:
        steps = jnp.exp(jax.random.uniform(jax.random.fold_in(own, dim), (parts,), jnp.float32, smallest / len(pieces), high / len(pieces)))
        level = level * jnp.repeat(steps, extent[dim] // parts).reshape([-1 if axis == dim else 1 for axis in range(len(extent))])
    return level


def normal_values(rng, shape, scale, limit, pieces=(), kind=jnp.bfloat16):
    level = block_scale(rng, shape, pieces, -0.22, 0.18) if pieces else 1.0
    entries = jax.random.normal(rng, shape, jnp.float32) * scale * level
    return jnp.minimum(jnp.maximum(entries, -limit), limit).astype(kind)


def setup_inputs(seed: int = 0) -> dict:
    key_list = jax.random.split(jax.random.key(seed), 11)
    return {
        "amplitudes": normal_values(key_list[0], (PAIRS, 8, VBLK * VBLK), 0.3, 4.0, ((0, 32),)),
        "slabs": normal_values(key_list[1], (SLOTS, 8, CWIN, VBLK, VBLK * VBLK), 0.1, 1.5, ((0, 32), (1, 8), (2, 2))),
        "couplings": normal_values(key_list[2], (K_WIN, NOCC, NOCC, CWIN * VBLK), 0.7, 6.0, ((3, 2),)),
        "occ_energy": jnp.clip(jax.random.uniform(key_list[3], (NOCC,), jnp.float32, -2.0, -0.3), -2.0, -0.3),
        "vir_energy": jnp.clip(jax.random.uniform(key_list[4], (8, VBLK), jnp.float32, 0.2, 4.0), 0.2, 4.0),
        "occ_irrep": with_ends(jax.random.randint(key_list[5], (NOCC,), 0, 8), jax.random.fold_in(key_list[5], 1), 0, 7).astype(jnp.int32),
        "pair_i": draw_pair_i(jax.random.fold_in(key_list[10], 71), 0),
        "pair_j": draw_pair_j(jax.random.fold_in(key_list[10], 71), 0),
        "window_k": jax.random.randint(key_list[8], (K_WIN,), 0, NOCC).astype(jnp.int32),
        "owner": jax.random.randint(key_list[9], (K_WIN,), 0, SLOTS).astype(jnp.int32),
    }


def reference(amplitudes, slabs, couplings, occ_energy, vir_energy, occ_irrep, pair_i, pair_j, window_k, owner):
    highest = lax.Precision.HIGHEST
    blocks = jnp.arange(8, dtype=jnp.int32)
    gammas = jnp.arange(CWIN, dtype=jnp.int32)
    pair_sym = jnp.bitwise_xor(occ_irrep[pair_i], occ_irrep[pair_j])
    selector = jnp.bitwise_xor(blocks[:, None], pair_sym[None, :])
    hole_amp = amplitudes[jnp.arange(PAIRS, dtype=jnp.int32)[None, :], selector].astype(jnp.float32)

    def one_pair(packed):
        amp_pair, occ_i, occ_j = packed
        pair_irrep = jnp.bitwise_xor(occ_irrep[occ_i], occ_irrep[occ_j])
        accumulated = jnp.zeros((8, VBLK * VBLK), jnp.float32)
        for window in range(K_WIN):
            k_index = window_k[window]
            k_irrep = occ_irrep[k_index]
            slab_data = jnp.take(slabs, owner[window], axis=0).astype(jnp.float32)
            alpha_irrep = jnp.bitwise_xor(jnp.bitwise_xor(pair_irrep, k_irrep), jnp.bitwise_xor(blocks[:, None], gammas[None, :]))
            amp_sel = amp_pair[alpha_irrep].reshape(8, CWIN, VBLK, VBLK).astype(jnp.float32)
            particle = jnp.einsum('bgad,bgdx->bgax', amp_sel, slab_data, precision=highest)
            y_column = jnp.take(couplings[window], occ_j, axis=1).reshape(NOCC, CWIN, VBLK)
            keep_mask = jnp.bitwise_xor(jnp.bitwise_xor(occ_irrep[:, None], gammas[None, :]), jnp.bitwise_xor(occ_irrep[occ_j], k_irrep)) == 0
            coef_rows = y_column.astype(jnp.float32) * keep_mask[:, :, None].astype(jnp.float32)
            coupling = (coef_rows[pair_j] * (pair_i == occ_i).astype(jnp.float32)[:, None, None]).astype(jnp.bfloat16)
            hole_part = jnp.einsum('bqx,qgc->bgxc', hole_amp, coupling.astype(jnp.float32), precision=highest)
            hole_part = hole_part.reshape(8, CWIN, VBLK, VBLK * VBLK)
            energy_a = vir_energy[alpha_irrep]
            energy_b = vir_energy
            energy_c = vir_energy[gammas]
            base = occ_energy[occ_i] + occ_energy[occ_j] + occ_energy[k_index]
            denominator = energy_a[:, :, :, None, None] + energy_b[:, None, None, :, None] + energy_c[None, :, None, None, :] - base
            triples = ((particle - hole_part) / denominator.reshape(8, CWIN, VBLK, VBLK * VBLK)).astype(jnp.bfloat16)
            contrib = jnp.einsum('bgax,bgdx->bgad', triples.astype(jnp.float32), slab_data, precision=highest)
            accumulated = accumulated.at[alpha_irrep.reshape(-1)].add(contrib.reshape(8 * CWIN, VBLK * VBLK))
        return accumulated

    return lax.map(one_pair, (amplitudes, pair_i, pair_j))
```

```python
import jax
import jax.numpy as jnp
from jax import lax
from jax.experimental import pallas as pl
from jax.experimental.pallas import tpu as pltpu
from jax.sharding import PartitionSpec as P

MESH = pl.DeviceIdType.MESH
YS, ZS, XS = 4, 8, 4
BLK = 88
PER = 5
NW = 2
BCH = BLK // YS
CHL = 2048
LAST = 7808
NCH = 8
CW = CHL // NCH
SKEW = 2
PACK = 896
OUTL = 512
ZSTEPS = (1, 2, 3, 4, -1, -2, -3)
VM = pl.BlockSpec(memory_space=pltpu.VMEM)
SM = pl.BlockSpec(memory_space=pltpu.SMEM)


def where_am_i():
    pair, vtile, irrep = lax.axis_index("pair"), lax.axis_index("vtile"), lax.axis_index("irrep")
    return pair, vtile, irrep, lax.rem(pair, YS), pair // YS


def spread_kernel(
    owner_ref, slab_ref, part_ref, hole_ref,
    vsel_ref, pall_ref, hall_ref,
    ybuf, frecv, brecv, fsend, bsend,
    ys_sem, yr_sem, hs_sem, hr_sem, ps_sem, pr_sem,
    fs_sem, fr_sem, bs_sem, br_sem, zs_sem, zr_sem, local_sem,
):
    pair, vtile, irrep, y, z = where_am_i()
    zg = irrep * ZS + z

    def at_y(k):
        ty = lax.rem(y + k + YS, YS)
        return ty, (z * YS + ty, vtile, irrep)

    def at_z(step):
        tz = lax.rem(zg + step + 2 * ZS, 2 * ZS)
        return (lax.rem(tz, ZS) * YS + y, vtile, tz // ZS)

    barrier = pltpu.get_barrier_semaphore()
    for k in (1, 2, 3):
        pl.semaphore_signal(barrier, inc=1, device_id=at_y(k)[1], device_id_type=MESH)
    for step in (1, 2, 3, 4, -1, -2, -3, -4):
        pl.semaphore_signal(barrier, inc=1, device_id=at_z(step), device_id_type=MESH)
    pl.semaphore_wait(barrier, 11)

    def hole_copy(k):
        ty, target = at_y(k)
        return pltpu.make_async_remote_copy(
            src_ref=hole_ref.at[ty], dst_ref=hall_ref.at[z, y],
            send_sem=hs_sem.at[k - 1], recv_sem=hr_sem.at[k - 1],
            device_id=target, device_id_type=MESH)

    def part_copy(k):
        _, target = at_y(k)
        return pltpu.make_async_remote_copy(
            src_ref=part_ref, dst_ref=pall_ref.at[y],
            send_sem=ps_sem.at[k - 1], recv_sem=pr_sem.at[k - 1],
            device_id=target, device_id_type=MESH)

    def slab_copy(k, n):
        ty, target = at_y(k)
        start = pl.multiple_of(ty * 1920 + n * CW, 128)
        return pltpu.make_async_remote_copy(
            src_ref=slab_ref.at[:, pl.ds(start, CW)],
            dst_ref=ybuf.at[y, :, pl.ds(pl.multiple_of(n * CW, CW), CW)],
            send_sem=ys_sem.at[k - 1, n], recv_sem=yr_sem.at[k - 1, n],
            device_id=target, device_id_type=MESH)

    def ring_copy(index):
        step = ZSTEPS[index]
        return pltpu.make_async_remote_copy(
            src_ref=hall_ref.at[z], dst_ref=hall_ref.at[z],
            send_sem=zs_sem.at[index], recv_sem=zr_sem.at[index],
            device_id=at_z(step), device_id_type=MESH)

    def chain_copy(forward, n):
        lanes = pl.ds(pl.multiple_of(n * CW, CW), CW)
        src, dst = (fsend, frecv) if forward else (bsend, brecv)
        send, recv = (fs_sem, fr_sem) if forward else (bs_sem, br_sem)
        tz = jnp.minimum(z + 1, ZS - 1) if forward else jnp.maximum(z - 1, 0)
        return pltpu.make_async_remote_copy(
            src_ref=src.at[:, :, lanes], dst_ref=dst.at[:, :, lanes],
            send_sem=send.at[n], recv_sem=recv.at[n],
            device_id=(tz * YS + y, vtile, irrep), device_id_type=MESH)

    for k in (1, 3, 2):
        hole_copy(k).start()

    def send_chunk(n, _):
        for k in (1, 3, 2):
            slab_copy(k, n).start()
        return 0

    lax.fori_loop(0, NCH, send_chunk, 0)
    for k in (1, 3, 2):
        part_copy(k).start()

    own_slab = pltpu.make_async_copy(
        slab_ref.at[:, pl.ds(pl.multiple_of(y * 1920, 128), CHL)], ybuf.at[y], local_sem.at[0])
    own_part = pltpu.make_async_copy(part_ref, pall_ref.at[y], local_sem.at[1])
    own_hole = pltpu.make_async_copy(hole_ref.at[y], hall_ref.at[z, y], local_sem.at[2])
    for copy in (own_slab, own_part, own_hole):
        copy.start()
    own_hole.wait()
    for k in (1, 2, 3):
        hole_copy(k).wait_recv()
    for index in (0, 4, 1, 5, 2, 6, 3):
        ring_copy(index).start()
    own_slab.wait()
    own_part.wait()

    root_y = [lax.rem(owner_ref[w], YS) for w in range(NW)]
    root_z = [owner_ref[w] // YS for w in range(NW)]

    def wait_y(n):
        for k in (1, 2, 3):
            slab_copy(k, n).wait_recv()

    def candidate(w, lanes):
        value = ybuf[0, :, lanes]
        for source in range(1, YS):
            value = jnp.where(root_y[w] == source, ybuf[source, :, lanes], value)
        return value

    def chain_event(forward, n):
        lanes = pl.ds(pl.multiple_of(n * CW, CW), CW)
        src, dst = (fsend, frecv) if forward else (bsend, brecv)
        first_here = z <= 3 if forward else z >= 4
        start, end = (z == 0, z == ZS - 1) if forward else (z == ZS - 1, z == 0)

        @pl.when(first_here)
        def _():
            wait_y(n)

        mine = [candidate(w, lanes) for w in range(NW)]

        @pl.when(start)
        def _():
            for w in range(NW):
                dst[w, :, lanes] = mine[w]

        @pl.when(jnp.logical_not(start))
        def _():
            chain_copy(forward, n).wait_recv()

        if forward:
            for w in range(NW):
                vsel_ref[w, :, lanes] = mine[w]

        @pl.when(jnp.logical_not(end))
        def _():
            for w in range(NW):
                src[w, :, lanes] = jnp.where(root_z[w] == z, mine[w], dst[w, :, lanes])
            chain_copy(forward, n).start()

    def chain_step(t, _):
        nf = t - SKEW * z
        nb = t - SKEW * (ZS - 1 - z)

        @pl.when(jnp.logical_and(nf >= 0, nf < NCH))
        def _():
            chain_event(True, nf)

        @pl.when(jnp.logical_and(nb >= 0, nb < NCH))
        def _():
            chain_event(False, nb)

        return 0

    lax.fori_loop(0, NCH + SKEW * (ZS - 1), chain_step, 0)

    def settle(n, _):
        lanes = pl.ds(pl.multiple_of(n * CW, CW), CW)
        for w in range(NW):
            other = jnp.where(root_z[w] < z, frecv[w, :, lanes], brecv[w, :, lanes])
            vsel_ref[w, :, lanes] = jnp.where(root_z[w] == z, vsel_ref[w, :, lanes], other)
        return 0

    lax.fori_loop(0, NCH, settle, 0)

    for k in (1, 2, 3):
        part_copy(k).wait_recv()
    for index in range(len(ZSTEPS)):
        tz = lax.rem(zg - ZSTEPS[index] + 2 * ZS, 2 * ZS)
        pltpu.make_async_remote_copy(
            src_ref=hall_ref.at[z], dst_ref=hall_ref.at[lax.rem(tz, ZS)],
            send_sem=zs_sem.at[index], recv_sem=zr_sem.at[index],
            device_id=at_z(ZSTEPS[index]), device_id_type=MESH).wait_recv()

    def sent(n, _):
        for k in (1, 2, 3):
            slab_copy(k, n).wait_send()

        @pl.when(z < ZS - 1)
        def _():
            chain_copy(True, n).wait_send()

        @pl.when(z > 0)
        def _():
            chain_copy(False, n).wait_send()

        return 0

    lax.fori_loop(0, NCH, sent, 0)
    for k in (1, 2, 3):
        hole_copy(k).wait_send()
        part_copy(k).wait_send()
    for index in range(len(ZSTEPS)):
        ring_copy(index).wait_send()


def window_of(offset, width):
    base = offset // 128 * 128
    return base, 128 if offset - base + width <= 128 else 256


def cut(value, offset):
    moved = pltpu.roll(value, value.shape[1] - offset, 1) if offset else value
    moved = moved[:, :128]
    lane = lax.broadcasted_iota(jnp.int32, moved.shape, 1)
    return jnp.where(lane < BLK, moved, 0.0)


def work_kernel(
    place_ref, first_ref, second_ref,
    hall_ref, vsel_ref, pall_ref, coup_ref, ea_ref, ebc_ref,
    out_ref,
    wide, left, vshift, vtile_ref, amp_ref, weight, holes, trip, column,
):
    y = place_ref[0]
    wide[...] = hall_ref[...].astype(jnp.float32)
    for k in range(16):
        tile = wide[pl.ds(k, 160, stride=16), :]
        left[128 * k:128 * k + 128, :] = tile.T.astype(jnp.bfloat16)
    table = wide[pl.ds(15, 160, stride=16), :]
    group, member = table[:, 16:17], table[:, 17:18]
    slot = lax.broadcasted_iota(jnp.int32, (160, 32), 1).astype(jnp.float32)
    for p in range(YS * PER):
        here = jnp.logical_and(member == slot, group == first_ref[p].astype(jnp.float32))
        pick = here.astype(jnp.float32).astype(jnp.bfloat16)
        both = jnp.dot(pick, coup_ref[second_ref[p]], preferred_element_type=jnp.float32)
        for w in range(NW):
            weight[w, :, 128 * p:128 * p + 128] = both[:, 128 * w:128 * w + 128].astype(jnp.bfloat16)

    for w in range(NW):
        for shift in range(YS):
            @pl.when(y == shift)
            def _():
                value = vsel_ref[w].astype(jnp.float32)
                vshift[...] = pltpu.roll(value, CHL - 16 * shift, 1) if shift else value
        for b in range(BCH):
            base, width = window_of(BLK * b, BLK)
            vtile_ref[:, 128 * b:128 * b + 128] = cut(
                vshift[:, base:base + width], BLK * b - base).astype(jnp.bfloat16)
        for source in range(YS):
            parts = []
            for p in range(PER):
                offset = BLK * (w * PER + p)
                base, width = window_of(offset, BLK)
                parts.append(cut(pall_ref[source, :, base:base + width].astype(jnp.float32), offset - base))
            amp_ref[source] = jnp.concatenate(parts, axis=0).astype(jnp.bfloat16)

        def hole_step(t, _):
            lanes = pl.ds(pl.multiple_of(t * 256, 256), 256)
            holes[:, lanes] = jnp.dot(
                left[:BCH * BLK, :], weight[w, :, lanes], preferred_element_type=jnp.float32)
            return 0

        lax.fori_loop(0, YS * PER // 2, hole_step, 0)

        def source_step(source, _):
            column[...] = jnp.broadcast_to(ea_ref[w * YS + source], (PER * BLK, 128))

            def tile_step(t, _):
                lanes = pl.ds(pl.multiple_of(t * 256, 256), 256)
                particle = jnp.dot(
                    amp_ref[source, :, :BLK], vtile_ref[:, lanes], preferred_element_type=jnp.float32)
                for half in range(2):
                    rows = pl.ds(pl.multiple_of((2 * t + half) * BLK, 8), BLK)
                    hole = jnp.concatenate([
                        holes[rows, pl.ds(pl.multiple_of((source * PER + p) * 128, 128), 128)]
                        for p in range(PER)], axis=0)
                    denominator = column[...] + ebc_ref[2 * t + half]
                    guess = pl.reciprocal(denominator, approx=True)
                    guess = guess * (2.0 - denominator * guess)
                    guess = guess * (2.0 - denominator * guess)
                    value = (particle[:, 128 * half:128 * half + 128] - hole) * guess
                    trip[source, :, pl.ds(pl.multiple_of(t * 256 + 128 * half, 128), 128)] = value.astype(jnp.bfloat16)
                return 0

            lax.fori_loop(0, BCH // 2, tile_step, 0)
            return 0

        lax.fori_loop(0, YS, source_step, 0)
        for source in range(YS):
            contrib = lax.dot_general(
                trip[source], vtile_ref[...], (((1,), (1,)), ((), ())), preferred_element_type=jnp.float32)
            for p in range(PER):
                offset = BLK * (w * PER + p)
                out_ref[source, :, offset:offset + BLK] = contrib[BLK * p:BLK * p + BLK]
    for source in range(YS):
        out_ref[source, :, 880:PACK] = jnp.zeros((BLK, PACK - 880), jnp.float32)


def sum_kernel(
    code_ref, c_ref, out_ref,
    ybuf, slots, cbuf, merged, xbuf, total, zbuf,
    ys_sem, yr_sem, cs_sem, cr_sem, xs_sem, xr_sem, zs_sem, zr_sem,
):
    pair, vtile, irrep, y, z = where_am_i()
    x, core = vtile // 2, lax.rem(vtile, 2)

    def at_y(k):
        ty = lax.rem(y + k, YS)
        return ty, (z * YS + ty, vtile, irrep)

    def at_x(k):
        tx = lax.rem(x + k, XS)
        return tx, (pair, tx * 2 + core, irrep)

    at_core = (pair, x * 2 + 1 - core, irrep)
    at_irrep = (pair, vtile, 1 - irrep)
    barrier = pltpu.get_barrier_semaphore()
    for k in (1, 2, 3):
        pl.semaphore_signal(barrier, inc=1, device_id=at_y(k)[1], device_id_type=MESH)
        pl.semaphore_signal(barrier, inc=1, device_id=at_x(k)[1], device_id_type=MESH)
    pl.semaphore_signal(barrier, inc=1, device_id=at_core, device_id_type=MESH)
    pl.semaphore_signal(barrier, inc=1, device_id=at_irrep, device_id_type=MESH)
    pl.semaphore_wait(barrier, 8)

    ycopies = []
    for k in (1, 3, 2):
        ty, target = at_y(k)
        ycopies.append(pltpu.make_async_remote_copy(
            src_ref=c_ref.at[ty], dst_ref=ybuf.at[k - 1],
            send_sem=ys_sem.at[k - 1], recv_sem=yr_sem.at[k - 1],
            device_id=target, device_id_type=MESH))
    for copy in ycopies:
        copy.start()
    for copy in ycopies:
        copy.wait()
    summed = c_ref[y] + ybuf[0] + ybuf[1] + ybuf[2]
    windows = [summed[:, :OUTL], pltpu.roll(summed, PACK - 440, 1)[:, :OUTL]]
    codes = [code_ref[w:w + 1, :] for w in range(NW)]
    for target in range(2 * XS):
        slots[target % 2, target // 2] = sum(
            jnp.where(codes[w] == target, windows[w], 0.0) for w in range(NW))
    ccopy = pltpu.make_async_remote_copy(
        src_ref=slots.at[1 - core], dst_ref=cbuf,
        send_sem=cs_sem, recv_sem=cr_sem, device_id=at_core, device_id_type=MESH)
    ccopy.start()
    ccopy.wait()
    for tx in range(XS):
        merged[tx] = slots[core, tx] + cbuf[tx]
    xcopies = []
    for k in (1, 3, 2):
        tx, target = at_x(k)
        xcopies.append(pltpu.make_async_remote_copy(
            src_ref=merged.at[tx], dst_ref=xbuf.at[k - 1],
            send_sem=xs_sem.at[k - 1], recv_sem=xr_sem.at[k - 1],
            device_id=target, device_id_type=MESH))
    for copy in xcopies:
        copy.start()
    for copy in xcopies:
        copy.wait()
    total[...] = merged[x] + xbuf[0] + xbuf[1] + xbuf[2]
    zcopy = pltpu.make_async_remote_copy(
        src_ref=total.at[pl.ds(pl.multiple_of(40 * (1 - irrep), 8), 48), :], dst_ref=zbuf,
        send_sem=zs_sem, recv_sem=zr_sem, device_id=at_irrep, device_id_type=MESH)
    zcopy.start()
    zcopy.wait()
    out_ref[...] = total[pl.ds(pl.multiple_of(40 * irrep, 8), 48), :] + zbuf[...]


DMA = pltpu.SemaphoreType.DMA


def spread_call(owner, slab, part, hole):
    half = jnp.bfloat16
    return pl.pallas_call(
        spread_kernel,
        out_shape=(
            jax.ShapeDtypeStruct((NW, BLK, CHL), half),
            jax.ShapeDtypeStruct((YS, BLK, PACK), half),
            jax.ShapeDtypeStruct((ZS, YS, 80, 128), half),
        ),
        in_specs=[SM, VM, VM, VM],
        out_specs=(VM, VM, VM),
        scratch_shapes=[
            pltpu.VMEM((YS, BLK, CHL), half),
            pltpu.VMEM((NW, BLK, CHL), half),
            pltpu.VMEM((NW, BLK, CHL), half),
            pltpu.VMEM((NW, BLK, CHL), half),
            pltpu.VMEM((NW, BLK, CHL), half),
            DMA((3, NCH)), DMA((3, NCH)), DMA((3,)), DMA((3,)), DMA((3,)), DMA((3,)),
            DMA((NCH,)), DMA((NCH,)), DMA((NCH,)), DMA((NCH,)), DMA((7,)), DMA((7,)), DMA((3,)),
        ],
        compiler_params=pltpu.CompilerParams(
            collective_id=0, has_side_effects=True, vmem_limit_bytes=40 * 2**20),
    )(owner, slab, part, hole)


def work_call(place, first, second, hall, vsel, pall, coup, ea, ebc):
    half = jnp.bfloat16
    return pl.pallas_call(
        work_kernel,
        out_shape=jax.ShapeDtypeStruct((YS, BLK, PACK), jnp.float32),
        in_specs=[SM, SM, SM] + [VM] * 6,
        out_specs=VM,
        scratch_shapes=[
            pltpu.VMEM((2560, 128), jnp.float32),
            pltpu.VMEM((CHL, 160), half),
            pltpu.VMEM((BLK, CHL), jnp.float32),
            pltpu.VMEM((BLK, 128 * BCH), half),
            pltpu.VMEM((YS, PER * BLK, 128), half),
            pltpu.VMEM((NW, 160, 128 * YS * PER), half),
            pltpu.VMEM((BCH * BLK, 128 * YS * PER), jnp.float32),
            pltpu.VMEM((YS, PER * BLK, 128 * BCH), half),
            pltpu.VMEM((PER * BLK, 128), jnp.float32),
        ],
        compiler_params=pltpu.CompilerParams(vmem_limit_bytes=56 * 2**20),
    )(place, first, second, hall, vsel, pall, coup, ea, ebc)


def sum_call(code, contrib):
    single = jnp.float32
    return pl.pallas_call(
        sum_kernel,
        out_shape=jax.ShapeDtypeStruct((48, OUTL), single),
        in_specs=[VM, VM],
        out_specs=VM,
        scratch_shapes=[
            pltpu.VMEM((3, BLK, PACK), single),
            pltpu.VMEM((2, XS, BLK, OUTL), single),
            pltpu.VMEM((XS, BLK, OUTL), single),
            pltpu.VMEM((XS, BLK, OUTL), single),
            pltpu.VMEM((3, BLK, OUTL), single),
            pltpu.VMEM((BLK, OUTL), single),
            pltpu.VMEM((48, OUTL), single),
            DMA((3,)), DMA((3,)), DMA, DMA, DMA((3,)), DMA((3,)), DMA, DMA,
        ],
        compiler_params=pltpu.CompilerParams(
            collective_id=1, has_side_effects=True, vmem_limit_bytes=40 * 2**20),
    )(code, contrib)


def on_device(
    amplitudes, slabs, couplings, occ_energy, vir_energy, occ_irrep, pair_i, pair_j, window_k, owner
):
    half = jnp.bfloat16
    pair, beta, gamma, y, z = where_am_i()
    k_irrep = occ_irrep[window_k]
    pair_sym = occ_irrep[pair_i] ^ occ_irrep[pair_j]
    local = jnp.arange(PER)
    alpha = pair_sym[None, :] ^ k_irrep[:, None] ^ beta ^ gamma
    index = jnp.concatenate([(beta ^ pair_sym)[:, None], alpha.T], axis=1)
    blocks = jnp.take_along_axis(amplitudes, index[:, :, None], axis=1).reshape(PER, 1 + NW, BLK, BLK)
    send = blocks[:, 0].swapaxes(1, 2).reshape(PER, YS, BCH * BLK)
    tags = jnp.stack([pair_i, pair_j], axis=1).astype(half)[:, None, :]
    tail = jnp.pad(jnp.broadcast_to(tags, (PER, YS, 2)), ((0, 0), (0, 0), (0, CHL - BCH * BLK - 2)))
    hole = jnp.concatenate([send, tail], axis=2).swapaxes(0, 1).reshape(YS, PER * 16, 128)
    part = blocks[:, 1:].transpose(2, 1, 0, 3).reshape(BLK, NW * PER * BLK)
    part = jnp.pad(part, ((0, 0), (0, PACK - NW * PER * BLK)))
    slab = jnp.pad(slabs.reshape(BLK, BLK * BLK), ((0, 0), (0, LAST - BLK * BLK)))
    vsel, pall, hall = spread_call(owner, slab, part, hole)

    table = lax.dynamic_index_in_dim(hall, z, 0, keepdims=False).reshape(YS * PER, 16, 128)[:, 15, 16:18]
    first, second = table[:, 0].astype(jnp.int32), table[:, 1].astype(jnp.int32)
    sym = occ_irrep[first] ^ occ_irrep[second]
    alphas = sym[None, :] ^ k_irrep[:, None] ^ beta ^ gamma
    base = (occ_energy[first] + occ_energy[second])[None, :] + occ_energy[window_k][:, None]
    ea = (vir_energy[alphas] - base[:, :, None]).reshape(NW * YS, PER * BLK, 1)
    eb = lax.dynamic_slice_in_dim(jnp.take(vir_energy, beta, axis=0), y * BCH, BCH, 0)
    ec = jnp.take(vir_energy, gamma, axis=0)
    ebc = jnp.pad(eb[:, None] + ec[None, :], ((0, 0), (0, 128 - BLK)), constant_values=20.0)[:, None, :]
    keep = occ_irrep[None, :, None] ^ gamma ^ occ_irrep[None, None, :] ^ k_irrep[:, None, None]
    coup = jnp.where((keep == 0)[..., None], couplings, jnp.zeros_like(couplings))
    coup = jnp.pad(coup, ((0, 0), (0, 2), (0, 0), (0, 128 - BLK))).transpose(2, 1, 0, 3).reshape(30, 32, 256)
    contrib = work_call(
        jnp.reshape(y, (1,)), first, second, hall.reshape(2560, 128), vsel, pall, coup, ea, ebc)
    code = jnp.repeat(alpha, BLK, axis=1)
    code = jnp.pad(code, ((0, 0), (0, OUTL - PER * BLK)), constant_values=-1)
    result = sum_call(code, contrib)
    result = lax.dynamic_slice_in_dim(result, 4 * gamma, BLK // 2, 0)[:, :PER * BLK]
    return result.reshape(BLK // 2, PER, BLK).swapaxes(0, 1).reshape(PER, 1, BLK * BLK // 2)


def solution(mesh):
    placed = (
        P("pair", None, None),
        P("pair", "vtile", "irrep", None, None),
        P(None, None, None, "irrep"),
        P(),
        P(),
        P(),
        P("pair"),
        P("pair"),
        P(),
        P(),
    )
    return jax.shard_map(
        on_device,
        mesh=mesh,
        in_specs=placed,
        out_specs=P("pair", "vtile", "irrep"),
        check_vma=False,
    )
```

```python
import jax
import jax.numpy as jnp
from jax import lax
from jax.experimental import pallas as pl
from jax.experimental.pallas import tpu as pltpu
from jax.sharding import PartitionSpec as P

MESH = pl.DeviceIdType.MESH
YS, ZS, XS = 4, 8, 4
BLK = 88
PER = 5
NW = 2
BCH = BLK // YS
CHL = 2048
TILES = 16
ALL = 61
YPER = 2
YN = TILES // YPER
SKEW = 4
RING = 8
RIGHT, LEFT = 4, 3
PACK = 896
OUTL = 512
VM = pl.BlockSpec(memory_space=pltpu.VMEM)
SM = pl.BlockSpec(memory_space=pltpu.SMEM)


def where_am_i():
    pair, vtile, irrep = lax.axis_index("pair"), lax.axis_index("vtile"), lax.axis_index("irrep")
    return pair, vtile, irrep, lax.rem(pair, YS), pair // YS


def spread_kernel(
    owner_ref, slab_ref, part_ref, hole_ref,
    vsel_ref, pall_ref, hall_ref,
    tiles, ybuf, frecv, brecv, fsend, bsend,
    ys_sem, yr_sem, hs_sem, hr_sem, ps_sem, pr_sem,
    fs_sem, fr_sem, bs_sem, br_sem, zs_sem, zr_sem, local_sem,
):
    pair, vtile, irrep, y, z = where_am_i()
    zg = irrep * ZS + z

    def at_y(k):
        ty = lax.rem(y + k + YS, YS)
        return ty, (z * YS + ty, vtile, irrep)

    def at_z(step):
        tz = lax.rem(zg + step + 2 * ZS, 2 * ZS)
        return (lax.rem(tz, ZS) * YS + y, vtile, tz // ZS)

    barrier = pltpu.get_barrier_semaphore()
    for k in (1, 2, 3):
        pl.semaphore_signal(barrier, inc=1, device_id=at_y(k)[1], device_id_type=MESH)
    for step in (1, -1):
        pl.semaphore_signal(barrier, inc=1, device_id=at_z(step), device_id_type=MESH)
    for t in range(ALL - 1):
        tiles[t] = slab_ref[:, 128 * t:128 * t + 128]
    tiles[ALL - 1] = jnp.zeros((BLK, 128), jnp.bfloat16)
    tiles[ALL - 1, :, :64] = slab_ref[:, 128 * (ALL - 1):]
    pl.semaphore_wait(barrier, 5)

    def hole_copy(k):
        ty, target = at_y(k)
        return pltpu.make_async_remote_copy(
            src_ref=hole_ref.at[ty], dst_ref=hall_ref.at[z, y],
            send_sem=hs_sem.at[k - 1], recv_sem=hr_sem.at[k - 1],
            device_id=target, device_id_type=MESH)

    def part_copy(k):
        _, target = at_y(k)
        return pltpu.make_async_remote_copy(
            src_ref=part_ref, dst_ref=pall_ref.at[y],
            send_sem=ps_sem.at[k - 1], recv_sem=pr_sem.at[k - 1],
            device_id=target, device_id_type=MESH)

    def slab_copy(k, n):
        ty, target = at_y(k)
        return pltpu.make_async_remote_copy(
            src_ref=tiles.at[pl.ds(ty * 15 + n * YPER, YPER)],
            dst_ref=ybuf.at[y, pl.ds(n * YPER, YPER)],
            send_sem=ys_sem.at[k - 1, n], recv_sem=yr_sem.at[k - 1, n],
            device_id=target, device_id_type=MESH)

    def ring_copy(index):
        step = index if index < RIGHT else index - RIGHT
        right = index < RIGHT
        held = lax.rem(zg + (-step if right else step) + 2 * ZS, ZS)
        return pltpu.make_async_remote_copy(
            src_ref=hall_ref.at[held], dst_ref=hall_ref.at[held],
            send_sem=zs_sem.at[index], recv_sem=zr_sem.at[index],
            device_id=at_z(1 if right else -1), device_id_type=MESH)

    def chain_copy(forward, n):
        src, dst = (fsend, frecv) if forward else (bsend, brecv)
        send, recv = (fs_sem, fr_sem) if forward else (bs_sem, br_sem)
        tz = jnp.minimum(z + 1, ZS - 1) if forward else jnp.maximum(z - 1, 0)
        return pltpu.make_async_remote_copy(
            src_ref=src.at[n], dst_ref=dst.at[n],
            send_sem=send.at[n], recv_sem=recv.at[n],
            device_id=(tz * YS + y, vtile, irrep), device_id_type=MESH)

    for k in (1, 3, 2):
        hole_copy(k).start()

    def send_chunk(n, _):
        for k in (1, 3, 2):
            slab_copy(k, n).start()
        return 0

    lax.fori_loop(0, YN, send_chunk, 0)
    for k in (1, 3, 2):
        part_copy(k).start()

    own_slab = pltpu.make_async_copy(tiles.at[pl.ds(y * 15, TILES)], ybuf.at[y], local_sem.at[0])
    own_part = pltpu.make_async_copy(part_ref, pall_ref.at[y], local_sem.at[1])
    own_hole = pltpu.make_async_copy(hole_ref.at[y], hall_ref.at[z, y], local_sem.at[2])
    for copy in (own_hole, own_slab, own_part):
        copy.start()
    own_hole.wait()
    for k in (1, 2, 3):
        hole_copy(k).wait_recv()
    ring_copy(0).start()
    ring_copy(RIGHT).start()
    own_slab.wait()
    own_part.wait()

    root_y = [lax.rem(owner_ref[w], YS) for w in range(NW)]
    root_z = [owner_ref[w] // YS for w in range(NW)]

    def candidate(w, n):
        value = ybuf[0, n]
        for source in range(1, YS):
            value = jnp.where(root_y[w] == source, ybuf[source, n], value)
        return value

    def chain_event(forward, n):
        src, dst = (fsend, frecv) if forward else (bsend, brecv)
        first_here = z <= 3 if forward else z >= 4
        start, end = (z == 0, z == ZS - 1) if forward else (z == ZS - 1, z == 0)

        @pl.when(jnp.logical_and(first_here, lax.rem(n, YPER) == 0))
        def _():
            for k in (1, 2, 3):
                slab_copy(k, n // YPER).wait_recv()

        mine = [candidate(w, n) for w in range(NW)]

        @pl.when(start)
        def _():
            for w in range(NW):
                dst[n, w] = mine[w]

        @pl.when(jnp.logical_not(start))
        def _():
            chain_copy(forward, n).wait_recv()

        if forward:
            for w in range(NW):
                vsel_ref[n, w] = mine[w]

        @pl.when(jnp.logical_not(end))
        def _():
            for w in range(NW):
                src[n, w] = jnp.where(root_z[w] == z, mine[w], dst[n, w])
            chain_copy(forward, n).start()

    def chain_step(t, _):
        nf = t - SKEW * z
        nb = t - SKEW * (ZS - 1 - z)

        @pl.when(jnp.logical_and(nf >= 0, nf < TILES))
        def _():
            chain_event(True, nf)

        @pl.when(jnp.logical_and(nb >= 0, nb < TILES))
        def _():
            chain_event(False, nb)

        for step in range(1, RIGHT):
            @pl.when(t == RING * step)
            def _():
                ring_copy(step - 1).wait_recv()
                ring_copy(step).start()
                if step < LEFT:
                    ring_copy(RIGHT + step - 1).wait_recv()
                    ring_copy(RIGHT + step).start()
        return 0

    lax.fori_loop(0, TILES + SKEW * (ZS - 1), chain_step, 0)

    def settle(n, _):
        for w in range(NW):
            other = jnp.where(root_z[w] < z, frecv[n, w], brecv[n, w])
            vsel_ref[n, w] = jnp.where(root_z[w] == z, vsel_ref[n, w], other)
        return 0

    lax.fori_loop(0, TILES, settle, 0)

    for k in (1, 2, 3):
        part_copy(k).wait_recv()
    ring_copy(RIGHT - 1).wait_recv()
    ring_copy(RIGHT + LEFT - 1).wait_recv()

    def sent(n, _):
        @pl.when(z < ZS - 1)
        def _():
            chain_copy(True, n).wait_send()

        @pl.when(z > 0)
        def _():
            chain_copy(False, n).wait_send()

        return 0

    lax.fori_loop(0, TILES, sent, 0)

    def sent_y(n, _):
        for k in (1, 2, 3):
            slab_copy(k, n).wait_send()
        return 0

    lax.fori_loop(0, YN, sent_y, 0)
    for k in (1, 2, 3):
        hole_copy(k).wait_send()
        part_copy(k).wait_send()
    for index in range(RIGHT + LEFT):
        ring_copy(index).wait_send()


def window_of(offset, width):
    base = offset // 128 * 128
    return base, 128 if offset - base + width <= 128 else 256


def cut(value, offset):
    moved = pltpu.roll(value, value.shape[1] - offset, 1) if offset else value
    moved = moved[:, :128]
    lane = lax.broadcasted_iota(jnp.int32, moved.shape, 1)
    return jnp.where(lane < BLK, moved, 0.0)


def work_kernel(
    first_ref, second_ref, irrep_ref, occ_ref, window_ref, vir_ref,
    hall_ref, vsel_ref, pall_ref, coup_ref, column_ref, row_ref,
    out_ref,
    wide, left, vshift, vt, vback, amp, weight, holes, column, acc,
    part0, part1, trip0, trip1, contrib,
    ybuf, slots, cbuf, merged, xbuf, total, zbuf,
    ys_sem, yr_sem, cs_sem, cr_sem, xs_sem, xr_sem, zs_sem, zr_sem,
):
    half, single = jnp.bfloat16, jnp.float32
    pair, vtile, irrep, y, z = where_am_i()
    x, core = vtile // 2, lax.rem(vtile, 2)

    def at_y(k):
        ty = lax.rem(y + k, YS)
        return ty, (z * YS + ty, vtile, irrep)

    def at_x(k):
        tx = lax.rem(x + k, XS)
        return tx, (pair, tx * 2 + core, irrep)

    at_core = (pair, x * 2 + 1 - core, irrep)
    at_irrep = (pair, vtile, 1 - irrep)
    barrier = pltpu.get_barrier_semaphore()
    for k in (1, 2, 3):
        pl.semaphore_signal(barrier, inc=1, device_id=at_y(k)[1], device_id_type=MESH)
        pl.semaphore_signal(barrier, inc=1, device_id=at_x(k)[1], device_id_type=MESH)
    pl.semaphore_signal(barrier, inc=1, device_id=at_core, device_id_type=MESH)
    pl.semaphore_signal(barrier, inc=1, device_id=at_irrep, device_id_type=MESH)

    wide[...] = hall_ref[...].astype(single)
    for k in range(16):
        tile = wide[pl.ds(k, 160, stride=16), :]
        left[128 * k:128 * k + 128, :] = tile.T.astype(half)
    table = wide[pl.ds(15, 160, stride=16), :]
    group, member = table[:, 16:17], table[:, 17:18]
    slot = lax.broadcasted_iota(jnp.int32, (160, 32), 1).astype(single)
    for p in range(YS * PER):
        here = jnp.logical_and(member == slot, group == first_ref[p].astype(single))
        pick = here.astype(single).astype(half)
        weight[:, 256 * p:256 * p + 256] = jnp.dot(
            pick, coup_ref[second_ref[p]], preferred_element_type=single).astype(half)

    for w in range(NW):
        for shift in range(YS):
            @pl.when(y == shift)
            def _():
                for t in range(TILES):
                    vshift[:, 128 * t:128 * t + 128] = vsel_ref[t, w].astype(single)
                if shift:
                    vshift[...] = pltpu.roll(vshift[...], CHL - 16 * shift, 1)
        for b in range(BCH):
            base, width = window_of(BLK * b, BLK)
            tile = cut(vshift[:, base:base + width], BLK * b - base)
            vt[w, :, 128 * b:128 * b + 128] = tile.astype(half)
            vback[w, 128 * b:128 * b + 128, :BLK] = tile.T.astype(half)
        for source in range(YS):
            parts = []
            for p in range(PER):
                offset = BLK * (w * PER + p)
                base, width = window_of(offset, BLK)
                parts.append(cut(pall_ref[source, :, base:base + width].astype(single), offset - base))
            amp[w, source] = jnp.concatenate(parts, axis=0).astype(half)
    vback[:, :, BLK:] = jnp.zeros((NW, 128 * BCH, 128 - BLK), half)
    contrib[:, :, 880:PACK] = jnp.zeros((YS, BLK, PACK - 880), single)
    pl.semaphore_wait(barrier, 8)

    def alpha_of(q, w):
        sym = irrep_ref[first_ref[q]] ^ irrep_ref[second_ref[q]]
        return sym ^ irrep_ref[window_ref[w]] ^ vtile ^ irrep

    def ycopy(k):
        ty, target = at_y(k)
        return pltpu.make_async_remote_copy(
            src_ref=contrib.at[ty], dst_ref=ybuf.at[k - 1],
            send_sem=ys_sem.at[k - 1], recv_sem=yr_sem.at[k - 1],
            device_id=target, device_id_type=MESH)

    gamma_row = row_ref[irrep]

    def source_step(index, _):
        source = lax.rem(y + index + 1, YS)

        def hole_step(p, _):
            lanes = pl.ds(pl.multiple_of(p * 256, 256), 256)
            mine = pl.ds(pl.multiple_of((source * PER + p) * 256, 256), 256)
            holes[:, lanes] = jnp.dot(left[:BCH * BLK, :], weight[:, mine], preferred_element_type=single)
            return 0

        lax.fori_loop(0, PER, hole_step, 0)
        for w in range(NW):
            for p in range(PER):
                q = source * PER + p
                base = occ_ref[first_ref[q]] + occ_ref[second_ref[q]] + occ_ref[window_ref[w]]
                column[BLK * p:BLK * p + BLK, :] = column_ref[alpha_of(q, w)] - base

            def lanes_of(t):
                return pl.ds(pl.multiple_of(t * 256, 256), 256)

            def particle(t):
                return jnp.dot(amp[w, source, :, :BLK], vt[w, :, lanes_of(t)], preferred_element_type=single)

            def stage(t, now, later, fill, drain):
                if later is not None:
                    later[...] = particle(t + 1)
                acc[...] += jnp.dot(
                    drain[...], vback[w, lanes_of(jnp.maximum(t - 1, 0)), :], preferred_element_type=single)
                for side in range(2):
                    b = 2 * t + side
                    rows = pl.ds(pl.multiple_of(b * BLK, 8), BLK)
                    hole = jnp.concatenate([
                        holes[rows, 256 * p + 128 * w:256 * p + 128 * w + 128] for p in range(PER)], axis=0)
                    energy = gamma_row + vir_ref[vtile, y * BCH + b]
                    inverse = pltpu.reciprocal(column[...] + energy, approx=True)
                    fill[:, 128 * side:128 * side + 128] = (
                        (now[:, 128 * side:128 * side + 128] - hole) * inverse).astype(half)

            acc[...] = jnp.zeros_like(acc)
            trip1[...] = jnp.zeros_like(trip1)
            part0[...] = particle(0)

            def two_steps(u, _):
                stage(2 * u, part0, part1, trip0, trip1)
                stage(2 * u + 1, part1, part0, trip1, trip0)
                return 0

            lax.fori_loop(0, BCH // 4, two_steps, 0)
            stage(BCH // 2 - 1, part0, None, trip0, trip1)
            acc[...] += jnp.dot(trip0[...], vback[w, 128 * (BCH - 2):, :], preferred_element_type=single)
            for p in range(PER):
                offset = BLK * (w * PER + p)
                contrib[source, :, offset:offset + BLK] = acc[BLK * p:BLK * p + BLK, :BLK]

        @pl.when(index < YS - 1)
        def _():
            ty, target = at_y(index + 1)
            pltpu.make_async_remote_copy(
                src_ref=contrib.at[ty], dst_ref=ybuf.at[index],
                send_sem=ys_sem.at[index], recv_sem=yr_sem.at[index],
                device_id=target, device_id_type=MESH).start()

        return 0

    lax.fori_loop(0, YS, source_step, 0)
    for k in (1, 2, 3):
        ycopy(k).wait()
    summed = contrib[y] + ybuf[0] + ybuf[1] + ybuf[2]
    windows = [summed[:, :OUTL], pltpu.roll(summed, PACK - 440, 1)[:, :OUTL]]
    lane = lax.broadcasted_iota(jnp.int32, (1, OUTL), 1)
    codes = []
    for w in range(NW):
        code = jnp.full((1, OUTL), -1, jnp.int32)
        for p in range(PER):
            inside = jnp.logical_and(lane >= BLK * p, lane < BLK * (p + 1))
            code = jnp.where(inside, alpha_of(y * PER + p, w), code)
        codes.append(code)
    for target in range(2 * XS):
        slots[target % 2, target // 2] = sum(
            jnp.where(codes[w] == target, windows[w], 0.0) for w in range(NW))
    ccopy = pltpu.make_async_remote_copy(
        src_ref=slots.at[1 - core], dst_ref=cbuf,
        send_sem=cs_sem, recv_sem=cr_sem, device_id=at_core, device_id_type=MESH)
    ccopy.start()
    ccopy.wait()
    for tx in range(XS):
        merged[tx] = slots[core, tx] + cbuf[tx]
    xcopies = []
    for k in (1, 3, 2):
        tx, target = at_x(k)
        xcopies.append(pltpu.make_async_remote_copy(
            src_ref=merged.at[tx], dst_ref=xbuf.at[k - 1],
            send_sem=xs_sem.at[k - 1], recv_sem=xr_sem.at[k - 1],
            device_id=target, device_id_type=MESH))
    for copy in xcopies:
        copy.start()
    for copy in xcopies:
        copy.wait()
    total[...] = merged[x] + xbuf[0] + xbuf[1] + xbuf[2]
    zcopy = pltpu.make_async_remote_copy(
        src_ref=total.at[pl.ds(pl.multiple_of(40 * (1 - irrep), 8), 48), :], dst_ref=zbuf,
        send_sem=zs_sem, recv_sem=zr_sem, device_id=at_irrep, device_id_type=MESH)
    zcopy.start()
    zcopy.wait()
    out_ref[...] = total[pl.ds(pl.multiple_of(40 * irrep, 8), 48), :] + zbuf[...]


DMA = pltpu.SemaphoreType.DMA


def spread_call(owner, slab, part, hole):
    half = jnp.bfloat16
    return pl.pallas_call(
        spread_kernel,
        out_shape=(
            jax.ShapeDtypeStruct((TILES, NW, BLK, 128), half),
            jax.ShapeDtypeStruct((YS, BLK, PACK), half),
            jax.ShapeDtypeStruct((ZS, YS, 80, 128), half),
        ),
        in_specs=[SM, VM, VM, VM],
        out_specs=(VM, VM, VM),
        scratch_shapes=[
            pltpu.VMEM((ALL, BLK, 128), half),
            pltpu.VMEM((YS, TILES, BLK, 128), half),
            pltpu.VMEM((TILES, NW, BLK, 128), half),
            pltpu.VMEM((TILES, NW, BLK, 128), half),
            pltpu.VMEM((TILES, NW, BLK, 128), half),
            pltpu.VMEM((TILES, NW, BLK, 128), half),
            DMA((3, YN)), DMA((3, YN)), DMA((3,)), DMA((3,)), DMA((3,)), DMA((3,)),
            DMA((TILES,)), DMA((TILES,)), DMA((TILES,)), DMA((TILES,)), DMA((7,)), DMA((7,)), DMA((3,)),
        ],
        compiler_params=pltpu.CompilerParams(
            collective_id=0, has_side_effects=True, vmem_limit_bytes=40 * 2**20),
    )(owner, slab, part, hole)


def work_call(first, second, irreps, occ, window, vir, hall, vsel, pall, coup, columns, rows):
    half, single = jnp.bfloat16, jnp.float32
    return pl.pallas_call(
        work_kernel,
        out_shape=jax.ShapeDtypeStruct((48, OUTL), single),
        in_specs=[SM] * 6 + [VM] * 6,
        out_specs=VM,
        scratch_shapes=[
            pltpu.VMEM((2560, 128), single),
            pltpu.VMEM((CHL, 160), half),
            pltpu.VMEM((BLK, CHL), single),
            pltpu.VMEM((NW, BLK, 128 * BCH), half),
            pltpu.VMEM((NW, 128 * BCH, 128), half),
            pltpu.VMEM((NW, YS, PER * BLK, 128), half),
            pltpu.VMEM((160, 256 * YS * PER), half),
            pltpu.VMEM((BCH * BLK, 256 * PER), single),
            pltpu.VMEM((PER * BLK, 128), single),
            pltpu.VMEM((PER * BLK, 128), single),
            pltpu.VMEM((PER * BLK, 256), single),
            pltpu.VMEM((PER * BLK, 256), single),
            pltpu.VMEM((PER * BLK, 256), half),
            pltpu.VMEM((PER * BLK, 256), half),
            pltpu.VMEM((YS, BLK, PACK), single),
            pltpu.VMEM((3, BLK, PACK), single),
            pltpu.VMEM((2, XS, BLK, OUTL), single),
            pltpu.VMEM((XS, BLK, OUTL), single),
            pltpu.VMEM((XS, BLK, OUTL), single),
            pltpu.VMEM((3, BLK, OUTL), single),
            pltpu.VMEM((BLK, OUTL), single),
            pltpu.VMEM((48, OUTL), single),
            DMA((3,)), DMA((3,)), DMA, DMA, DMA((3,)), DMA((3,)), DMA, DMA,
        ],
        compiler_params=pltpu.CompilerParams(
            collective_id=1, has_side_effects=True, vmem_limit_bytes=56 * 2**20),
    )(first, second, irreps, occ, window, vir, hall, vsel, pall, coup, columns, rows)


def pick(table, index):
    places = jnp.arange(table.shape[0], dtype=jnp.int32)
    return jnp.sum(jnp.where(index[..., None] == places, table, 0), axis=-1)


def on_device(
    amplitudes, slabs, couplings, occ_energy, vir_energy, occ_irrep, pair_i, pair_j, window_k, owner
):
    half = jnp.bfloat16
    pair, beta, gamma, y, z = where_am_i()
    k_irrep = pick(occ_irrep, window_k)
    pair_sym = pick(occ_irrep, pair_i) ^ pick(occ_irrep, pair_j)
    alpha = pair_sym[None, :] ^ k_irrep[:, None] ^ beta ^ gamma
    index = jnp.concatenate([(beta ^ pair_sym)[:, None], alpha.T], axis=1)
    blocks = jnp.take_along_axis(amplitudes, index[:, :, None], axis=1).reshape(PER, 1 + NW, BLK, BLK)
    send = blocks[:, 0].swapaxes(1, 2).reshape(PER, YS, BCH * BLK)
    tags = jnp.stack([pair_i, pair_j], axis=1).astype(half)[:, None, :]
    tail = jnp.pad(jnp.broadcast_to(tags, (PER, YS, 2)), ((0, 0), (0, 0), (0, CHL - BCH * BLK - 2)))
    hole = jnp.concatenate([send, tail], axis=2).swapaxes(0, 1).reshape(YS, PER * 16, 128)
    part = blocks[:, 1:].transpose(2, 1, 0, 3).reshape(BLK, NW * PER * BLK)
    part = jnp.pad(part, ((0, 0), (0, PACK - NW * PER * BLK)))
    vsel, pall, hall = spread_call(owner, slabs.reshape(BLK, BLK * BLK), part, hole)

    table = lax.dynamic_index_in_dim(hall, z, 0, keepdims=False).reshape(YS * PER, 16, 128)[:, 15, 16:18]
    first, second = table[:, 0].astype(jnp.int32), table[:, 1].astype(jnp.int32)
    columns = jnp.broadcast_to(vir_energy[:, :, None], (8, BLK, 128))
    rows = jnp.pad(vir_energy, ((0, 0), (0, 128 - BLK)), constant_values=20.0)[:, None, :]
    keep = occ_irrep[None, :, None] ^ gamma ^ occ_irrep[None, None, :] ^ k_irrep[:, None, None]
    coup = jnp.where((keep == 0)[..., None], couplings, jnp.zeros_like(couplings))
    coup = jnp.pad(coup, ((0, 0), (0, 2), (0, 0), (0, 128 - BLK))).transpose(2, 1, 0, 3).reshape(30, 32, 256)
    result = work_call(
        first, second, occ_irrep, occ_energy, window_k, vir_energy,
        hall.reshape(2560, 128), vsel, pall, coup, columns, rows)
    result = lax.dynamic_slice_in_dim(result, 4 * gamma, BLK // 2, 0)[:, :PER * BLK]
    return result.reshape(BLK // 2, PER, BLK).swapaxes(0, 1).reshape(PER, 1, BLK * BLK // 2)


def solution(mesh):
    placed = (
        P("pair", None, None),
        P("pair", "vtile", "irrep", None, None),
        P(None, None, None, "irrep"),
        P(),
        P(),
        P(),
        P("pair"),
        P("pair"),
        P(),
        P(),
    )
    return jax.shard_map(
        on_device,
        mesh=mesh,
        in_specs=placed,
        out_specs=P("pair", "vtile", "irrep"),
        check_vma=False,
    )
```

```python
import jax
import jax.numpy as jnp
from jax import lax
from jax.experimental import pallas as pl
from jax.experimental.pallas import tpu as pltpu
from jax.sharding import PartitionSpec as P

MESH = pl.DeviceIdType.MESH
YS, ZS, XS = 4, 8, 4
BLK = 88
PER = 5
NW = 2
BCH = BLK // YS
CHL = 2048
TILES = 16
ALL = 61
YPER = 2
YN = TILES // YPER
SKEW = 4
RING = 4
WEIGHTS = RING * 4 + 5
HOLES = WEIGHTS + 4
RIGHT, LEFT = 4, 3
PACK = 896
OUTL = 512
VM = pl.BlockSpec(memory_space=pltpu.VMEM)
SM = pl.BlockSpec(memory_space=pltpu.SMEM)


def where_am_i():
    pair, vtile, irrep = lax.axis_index("pair"), lax.axis_index("vtile"), lax.axis_index("irrep")
    return pair, vtile, irrep, lax.rem(pair, YS), pair // YS


def window_of(offset, width):
    base = offset // 128 * 128
    return base, 128 if offset - base + width <= 128 else 256


def cut(value, offset):
    moved = pltpu.roll(value, value.shape[1] - offset, 1) if offset else value
    moved = moved[:, :128]
    lane = lax.broadcasted_iota(jnp.int32, moved.shape, 1)
    return jnp.where(lane < BLK, moved, 0.0)


def kernel(
    owner_ref, irrep_ref, occ_ref, window_ref, vir_ref,
    slab_ref, part_ref, hole_ref, coup_ref, column_ref, row_ref, table_ref,
    out_ref,
    tiles, ybuf, frecv, brecv, fsend, bsend, pall_ref, hall_ref,
    own, ystage, alphas, bases,
    wide, left, vshift, vt, vback, amp, weight, holes, column, acc,
    part0, part1, trip0, trip1, contrib,
    rbuf, slots, cbuf, merged, xbuf, total, zbuf,
    ys_sem, yr_sem, hs_sem, hr_sem, ps_sem, pr_sem,
    fs_sem, fr_sem, bs_sem, br_sem, zs_sem, zr_sem, local_sem,
    rs_sem, rr_sem, cs_sem, cr_sem, xs_sem, xr_sem, ts_sem, tr_sem,
):
    half, single = jnp.bfloat16, jnp.float32
    pair, vtile, irrep, y, z = where_am_i()
    x, core = vtile // 2, lax.rem(vtile, 2)
    zg = irrep * ZS + z

    def at_y(k):
        ty = lax.rem(y + k + YS, YS)
        return ty, (z * YS + ty, vtile, irrep)

    def at_z(step):
        tz = lax.rem(zg + step + 2 * ZS, 2 * ZS)
        return (lax.rem(tz, ZS) * YS + y, vtile, tz // ZS)

    def at_x(k):
        tx = lax.rem(x + k, XS)
        return tx, (pair, tx * 2 + core, irrep)

    at_core = (pair, x * 2 + 1 - core, irrep)
    at_irrep = (pair, vtile, 1 - irrep)
    barrier = pltpu.get_barrier_semaphore()
    for k in (1, 2, 3):
        pl.semaphore_signal(barrier, inc=1, device_id=at_y(k)[1], device_id_type=MESH)
        pl.semaphore_signal(barrier, inc=1, device_id=at_x(k)[1], device_id_type=MESH)
    pl.semaphore_signal(barrier, inc=1, device_id=at_core, device_id_type=MESH)
    pl.semaphore_signal(barrier, inc=1, device_id=at_irrep, device_id_type=MESH)
    for step in (1, -1):
        pl.semaphore_signal(barrier, inc=1, device_id=at_z(step), device_id_type=MESH)
    for t in range(ALL - 1):
        tiles[t] = slab_ref[:, 128 * t:128 * t + 128]
    tiles[ALL - 1] = jnp.zeros((BLK, 128), jnp.bfloat16)
    tiles[ALL - 1, :, :64] = slab_ref[:, 128 * (ALL - 1):]
    pl.semaphore_wait(barrier, 10)

    def hole_copy(k):
        ty, target = at_y(k)
        return pltpu.make_async_remote_copy(
            src_ref=hole_ref.at[ty], dst_ref=hall_ref.at[z, y],
            send_sem=hs_sem.at[k - 1], recv_sem=hr_sem.at[k - 1],
            device_id=target, device_id_type=MESH)

    def part_copy(k):
        _, target = at_y(k)
        return pltpu.make_async_remote_copy(
            src_ref=part_ref, dst_ref=pall_ref.at[y],
            send_sem=ps_sem.at[k - 1], recv_sem=pr_sem.at[k - 1],
            device_id=target, device_id_type=MESH)

    def slab_copy(k, n):
        ty, target = at_y(k)
        return pltpu.make_async_remote_copy(
            src_ref=tiles.at[pl.ds(ty * 15 + n * YPER, YPER)],
            dst_ref=ybuf.at[y, pl.ds(n * YPER, YPER)],
            send_sem=ys_sem.at[k - 1, n], recv_sem=yr_sem.at[k - 1, n],
            device_id=target, device_id_type=MESH)

    def ring_copy(index):
        step = index if index < RIGHT else index - RIGHT
        right = index < RIGHT
        held = lax.rem(zg + (-step if right else step) + 2 * ZS, ZS)
        return pltpu.make_async_remote_copy(
            src_ref=hall_ref.at[held], dst_ref=hall_ref.at[held],
            send_sem=zs_sem.at[index], recv_sem=zr_sem.at[index],
            device_id=at_z(1 if right else -1), device_id_type=MESH)

    def chain_copy(forward, n):
        src, dst = (fsend, frecv) if forward else (bsend, brecv)
        send, recv = (fs_sem, fr_sem) if forward else (bs_sem, br_sem)
        tz = jnp.minimum(z + 1, ZS - 1) if forward else jnp.maximum(z - 1, 0)
        return pltpu.make_async_remote_copy(
            src_ref=src.at[n], dst_ref=dst.at[n],
            send_sem=send.at[n], recv_sem=recv.at[n],
            device_id=(tz * YS + y, vtile, irrep), device_id_type=MESH)

    for k in (1, 3, 2):
        hole_copy(k).start()

    def send_chunk(n, _):
        for k in (1, 3, 2):
            slab_copy(k, n).start()
        return 0

    lax.fori_loop(0, YN, send_chunk, 0)
    for k in (1, 3, 2):
        part_copy(k).start()

    own_slab = pltpu.make_async_copy(tiles.at[pl.ds(y * 15, TILES)], ybuf.at[y], local_sem.at[0])
    own_part = pltpu.make_async_copy(part_ref, pall_ref.at[y], local_sem.at[1])
    own_hole = pltpu.make_async_copy(hole_ref.at[y], hall_ref.at[z, y], local_sem.at[2])
    for copy in (own_hole, own_slab, own_part):
        copy.start()
    own_hole.wait()
    for k in (1, 2, 3):
        hole_copy(k).wait_recv()
    ring_copy(0).start()
    ring_copy(RIGHT).start()
    own_slab.wait()
    own_part.wait()

    mine_f = hall_ref[z].astype(single)
    for source in range(YS):
        own[80 * source:80 * source + 80, :] = mine_f[source]
    pairs = own[pl.ds(15, YS * PER, stride=16), :]
    lane20 = lax.broadcasted_iota(jnp.int32, (YS * PER, 128), 1).astype(single)
    is_first, is_second = pairs[:, 16:17] == lane20, pairs[:, 17:18] == lane20

    def look(mask, row):
        return jnp.sum(jnp.where(mask, table_ref[row:row + 1, :], 0.0), axis=1, keepdims=True)

    sym = look(is_first, 0).astype(jnp.int32) ^ look(is_second, 0).astype(jnp.int32)
    energy2 = look(is_first, 1) + look(is_second, 1)
    for w in range(NW):
        shift = irrep_ref[window_ref[w]] ^ vtile ^ irrep
        alphas[w] = jnp.broadcast_to(sym ^ shift, (YS * PER, 128))
        bases[w] = jnp.broadcast_to(energy2 + occ_ref[window_ref[w]], (YS * PER, 128))
    choose = is_second.astype(single)[:, :32].astype(half)
    ystage[:, 24 * 30:, :] = jnp.zeros((NW, 48, 128), single)
    for l in range(30):
        both = jnp.dot(choose, coup_ref[l], preferred_element_type=single)
        for w in range(NW):
            ystage[w, 24 * l:24 * l + YS * PER, :] = both[:, 128 * w:128 * w + 128]

    root_y = [lax.rem(owner_ref[w], YS) for w in range(NW)]
    root_z = [owner_ref[w] // YS for w in range(NW)]

    def candidate(w, n):
        value = ybuf[0, n]
        for source in range(1, YS):
            value = jnp.where(root_y[w] == source, ybuf[source, n], value)
        return value

    def chain_event(forward, n):
        src, dst = (fsend, frecv) if forward else (bsend, brecv)
        first_here = z <= 3 if forward else z >= 4
        start, end = (z == 0, z == ZS - 1) if forward else (z == ZS - 1, z == 0)

        @pl.when(jnp.logical_and(first_here, lax.rem(n, YPER) == 0))
        def _():
            for k in (1, 2, 3):
                slab_copy(k, n // YPER).wait_recv()

        mine = [candidate(w, n) for w in range(NW)]

        @pl.when(start)
        def _():
            for w in range(NW):
                dst[n, w] = mine[w]

        @pl.when(jnp.logical_not(start))
        def _():
            chain_copy(forward, n).wait_recv()

        @pl.when(jnp.logical_not(end))
        def _():
            for w in range(NW):
                src[n, w] = jnp.where(root_z[w] == z, mine[w], dst[n, w])
            chain_copy(forward, n).start()

    def hole_unit(index, p, place):
        source = lax.rem(y + index + 1, YS)
        lanes = pl.ds(pl.multiple_of(p * 256, 256), 256)
        holes[place, :, lanes] = jnp.dot(
            left[:BCH * BLK, :], weight[source, :, lanes], preferred_element_type=single)

    def chain_step(t, _):
        nf = t - SKEW * z
        nb = t - SKEW * (ZS - 1 - z)

        @pl.when(jnp.logical_and(nf >= 0, nf < TILES))
        def _():
            chain_event(True, nf)

        @pl.when(jnp.logical_and(nb >= 0, nb < TILES))
        def _():
            chain_event(False, nb)

        for step in range(1, RIGHT):
            @pl.when(t == RING * step)
            def _():
                ring_copy(step - 1).wait_recv()
                ring_copy(step).start()
                if step < LEFT:
                    ring_copy(RIGHT + step - 1).wait_recv()
                    ring_copy(RIGHT + step).start()
        @pl.when(t == RING * RIGHT)
        def _():
            ring_copy(RIGHT - 1).wait_recv()
            ring_copy(RIGHT + LEFT - 1).wait_recv()
            for block in range(ZS * YS):
                wide[80 * block:80 * block + 80, :] = hall_ref[block // YS, block % YS].astype(single)

        for quarter in range(4):
            @pl.when(t == RING * RIGHT + 1 + quarter)
            def _():
                for k in range(4 * quarter, 4 * quarter + 4):
                    tile = wide[pl.ds(k, 160, stride=16), :]
                    left[128 * k:128 * k + 128, :] = tile.T.astype(half)

        @pl.when(jnp.logical_and(t >= WEIGHTS, t < WEIGHTS + YS))
        def _():
            source = t - WEIGHTS
            table = wide[pl.ds(15, 160, stride=16), :]
            slot = lax.broadcasted_iota(jnp.int32, (160, 32), 1).astype(single)
            member = table[:, 17:18] == slot
            for p in range(PER):
                row = own[pl.ds(80 * source + 16 * p + 15, 1), :]
                here = jnp.logical_and(member, table[:, 16:17] == row[:, 16:17])
                rows = jnp.concatenate(
                    [ystage[w, pl.ds(source * PER + p, 32, stride=24), :] for w in range(NW)], axis=1)
                weight[source, :, 256 * p:256 * p + 256] = jnp.dot(
                    here.astype(single).astype(half), rows.astype(half), preferred_element_type=single).astype(half)

        @pl.when(jnp.logical_and(t >= HOLES, t < HOLES + 3 * PER))
        def _():
            hole_unit((t - HOLES) // PER, lax.rem(t - HOLES, PER), (t - HOLES) // PER)

        return 0

    lax.fori_loop(0, TILES + SKEW * (ZS - 1), chain_step, 0)

    for k in (1, 2, 3):
        part_copy(k).wait_recv()
    for w in range(NW):
        for t in range(TILES):
            other = jnp.where(root_z[w] < z, frecv[t, w], brecv[t, w])
            vshift[:, 128 * t:128 * t + 128] = jnp.where(
                root_z[w] == z, candidate(w, t), other).astype(single)
        for shift in range(1, YS):
            @pl.when(y == shift)
            def _():
                if shift:
                    vshift[...] = pltpu.roll(vshift[...], CHL - 16 * shift, 1)
        for b in range(BCH):
            base, width = window_of(BLK * b, BLK)
            tile = cut(vshift[:, base:base + width], BLK * b - base)
            vt[w, :, 128 * b:128 * b + 128] = tile.astype(half)
            vback[w, 128 * b:128 * b + 128, :BLK] = tile.T.astype(half)
        for source in range(YS):
            parts = []
            for p in range(PER):
                offset = BLK * (w * PER + p)
                base, width = window_of(offset, BLK)
                parts.append(cut(pall_ref[source, :, base:base + width].astype(single), offset - base))
            amp[w, source] = jnp.concatenate(parts, axis=0).astype(half)
    vback[:, :, BLK:] = jnp.zeros((NW, 128 * BCH, 128 - BLK), half)
    contrib[:, :, 880:PACK] = jnp.zeros((YS, BLK, PACK - 880), single)
    def ycopy(k):
        ty, target = at_y(k)
        return pltpu.make_async_remote_copy(
            src_ref=contrib.at[ty], dst_ref=rbuf.at[k - 1],
            send_sem=rs_sem.at[k - 1], recv_sem=rr_sem.at[k - 1],
            device_id=target, device_id_type=MESH)

    gamma_row = row_ref[irrep]

    def source_step(index, _):
        source = lax.rem(y + index + 1, YS)

        place = lax.rem(index, 3)

        @pl.when(index == YS - 1)
        def _():
            def hole_step(p, _):
                hole_unit(YS - 1, p, 0)
                return 0

            lax.fori_loop(0, PER, hole_step, 0)

        for w in range(NW):
            for p in range(PER):
                here = pl.ds(source * PER + p, 1)
                alpha, energy = alphas[w, here, :], column_ref[0]
                for h in range(1, 8):
                    energy = jnp.where(alpha == h, column_ref[h], energy)
                column[BLK * p:BLK * p + BLK, :] = energy - bases[w, here, :]

            def lanes_of(t):
                return pl.ds(pl.multiple_of(t * 256, 256), 256)

            def particle(t):
                return jnp.dot(amp[w, source, :, :BLK], vt[w, :, lanes_of(t)], preferred_element_type=single)

            def stage(t, now, later, fill, drain):
                if later is not None:
                    later[...] = particle(t + 1)
                acc[...] += jnp.dot(
                    drain[...], vback[w, lanes_of(jnp.maximum(t - 1, 0)), :], preferred_element_type=single)
                for side in range(2):
                    b = 2 * t + side
                    rows = pl.ds(pl.multiple_of(b * BLK, 8), BLK)
                    hole = jnp.concatenate([
                        holes[place, rows, 256 * p + 128 * w:256 * p + 128 * w + 128] for p in range(PER)], axis=0)
                    energy = gamma_row + vir_ref[vtile, y * BCH + b]
                    inverse = pltpu.reciprocal(column[...] + energy, approx=True)
                    fill[:, 128 * side:128 * side + 128] = (
                        (now[:, 128 * side:128 * side + 128] - hole) * inverse).astype(half)

            acc[...] = jnp.zeros_like(acc)
            trip1[...] = jnp.zeros_like(trip1)
            part0[...] = particle(0)

            def two_steps(u, _):
                stage(2 * u, part0, part1, trip0, trip1)
                stage(2 * u + 1, part1, part0, trip1, trip0)
                return 0

            lax.fori_loop(0, BCH // 4, two_steps, 0)
            stage(BCH // 2 - 1, part0, None, trip0, trip1)
            acc[...] += jnp.dot(trip0[...], vback[w, 128 * (BCH - 2):, :], preferred_element_type=single)
            for p in range(PER):
                offset = BLK * (w * PER + p)
                contrib[source, :, offset:offset + BLK] = acc[BLK * p:BLK * p + BLK, :BLK]

        @pl.when(index < YS - 1)
        def _():
            ty, target = at_y(index + 1)
            pltpu.make_async_remote_copy(
                src_ref=contrib.at[ty], dst_ref=rbuf.at[index],
                send_sem=rs_sem.at[index], recv_sem=rr_sem.at[index],
                device_id=target, device_id_type=MESH).start()

        return 0

    lax.fori_loop(0, YS, source_step, 0)
    for k in (1, 2, 3):
        ycopy(k).wait()
    summed = contrib[y] + rbuf[0] + rbuf[1] + rbuf[2]
    windows = [summed[:, :OUTL], pltpu.roll(summed, PACK - 440, 1)[:, :OUTL]]
    lane = lax.broadcasted_iota(jnp.int32, (1, OUTL), 1)
    codes = []
    for w in range(NW):
        code = jnp.full((1, OUTL), -1, jnp.int32)
        for p in range(PER):
            inside = jnp.logical_and(lane >= BLK * p, lane < BLK * (p + 1))
            alpha = jnp.concatenate([alphas[w, pl.ds(y * PER + p, 1), :]] * 4, axis=1)
            code = jnp.where(inside, alpha, code)
        codes.append(code)
    for target in range(2 * XS):
        slots[target % 2, target // 2] = sum(
            jnp.where(codes[w] == target, windows[w], 0.0) for w in range(NW))
    ccopy = pltpu.make_async_remote_copy(
        src_ref=slots.at[1 - core], dst_ref=cbuf,
        send_sem=cs_sem, recv_sem=cr_sem, device_id=at_core, device_id_type=MESH)
    ccopy.start()
    ccopy.wait()
    for tx in range(XS):
        merged[tx] = slots[core, tx] + cbuf[tx]
    xcopies = []
    for k in (1, 3, 2):
        tx, target = at_x(k)
        xcopies.append(pltpu.make_async_remote_copy(
            src_ref=merged.at[tx], dst_ref=xbuf.at[k - 1],
            send_sem=xs_sem.at[k - 1], recv_sem=xr_sem.at[k - 1],
            device_id=target, device_id_type=MESH))
    for copy in xcopies:
        copy.start()
    for copy in xcopies:
        copy.wait()
    total[...] = merged[x] + xbuf[0] + xbuf[1] + xbuf[2]
    zcopy = pltpu.make_async_remote_copy(
        src_ref=total.at[pl.ds(pl.multiple_of(40 * (1 - irrep), 8), 48), :], dst_ref=zbuf,
        send_sem=ts_sem, recv_sem=tr_sem, device_id=at_irrep, device_id_type=MESH)
    zcopy.start()
    def sent(n, _):
        @pl.when(z < ZS - 1)
        def _():
            chain_copy(True, n).wait_send()

        @pl.when(z > 0)
        def _():
            chain_copy(False, n).wait_send()

        return 0

    lax.fori_loop(0, TILES, sent, 0)

    def sent_y(n, _):
        for k in (1, 2, 3):
            slab_copy(k, n).wait_send()
        return 0

    lax.fori_loop(0, YN, sent_y, 0)
    for k in (1, 2, 3):
        hole_copy(k).wait_send()
        part_copy(k).wait_send()
    for index in range(RIGHT + LEFT):
        ring_copy(index).wait_send()
    zcopy.wait()
    out_ref[...] = total[pl.ds(pl.multiple_of(40 * irrep, 8), 48), :] + zbuf[...]


DMA = pltpu.SemaphoreType.DMA


def call(*operands):
    half, single = jnp.bfloat16, jnp.float32
    return pl.pallas_call(
        kernel,
        out_shape=jax.ShapeDtypeStruct((48, OUTL), single),
        in_specs=[SM] * 5 + [VM] * 7,
        out_specs=VM,
        scratch_shapes=[
            pltpu.VMEM((ALL, BLK, 128), half),
            pltpu.VMEM((YS, TILES, BLK, 128), half),
            pltpu.VMEM((TILES, NW, BLK, 128), half),
            pltpu.VMEM((TILES, NW, BLK, 128), half),
            pltpu.VMEM((TILES, NW, BLK, 128), half),
            pltpu.VMEM((TILES, NW, BLK, 128), half),
            pltpu.VMEM((YS, BLK, PACK), half),
            pltpu.VMEM((ZS, YS, 80, 128), half),
            pltpu.VMEM((YS * 80, 128), single),
            pltpu.VMEM((NW, 24 * 32, 128), single),
            pltpu.VMEM((NW, YS * PER, 128), jnp.int32),
            pltpu.VMEM((NW, YS * PER, 128), single),
            pltpu.VMEM((2560, 128), single),
            pltpu.VMEM((CHL, 160), half),
            pltpu.VMEM((BLK, CHL), single),
            pltpu.VMEM((NW, BLK, 128 * BCH), half),
            pltpu.VMEM((NW, 128 * BCH, 128), half),
            pltpu.VMEM((NW, YS, PER * BLK, 128), half),
            pltpu.VMEM((YS, 160, 256 * PER), half),
            pltpu.VMEM((3, BCH * BLK, 256 * PER), single),
            pltpu.VMEM((PER * BLK, 128), single),
            pltpu.VMEM((PER * BLK, 128), single),
            pltpu.VMEM((PER * BLK, 256), single),
            pltpu.VMEM((PER * BLK, 256), single),
            pltpu.VMEM((PER * BLK, 256), half),
            pltpu.VMEM((PER * BLK, 256), half),
            pltpu.VMEM((YS, BLK, PACK), single),
            pltpu.VMEM((3, BLK, PACK), single),
            pltpu.VMEM((2, XS, BLK, OUTL), single),
            pltpu.VMEM((XS, BLK, OUTL), single),
            pltpu.VMEM((XS, BLK, OUTL), single),
            pltpu.VMEM((3, BLK, OUTL), single),
            pltpu.VMEM((BLK, OUTL), single),
            pltpu.VMEM((48, OUTL), single),
            DMA((3, YN)), DMA((3, YN)), DMA((3,)), DMA((3,)), DMA((3,)), DMA((3,)),
            DMA((TILES,)), DMA((TILES,)), DMA((TILES,)), DMA((TILES,)), DMA((7,)), DMA((7,)), DMA((3,)),
            DMA((3,)), DMA((3,)), DMA, DMA, DMA((3,)), DMA((3,)), DMA, DMA,
        ],
        compiler_params=pltpu.CompilerParams(
            collective_id=0, has_side_effects=True, vmem_limit_bytes=62 * 2**20),
    )(*operands)


def pick(table, index):
    places = jnp.arange(table.shape[0], dtype=jnp.int32)
    return jnp.sum(jnp.where(index[..., None] == places, table, 0), axis=-1)


def on_device(
    amplitudes, slabs, couplings, occ_energy, vir_energy, occ_irrep, pair_i, pair_j, window_k, owner
):
    half = jnp.bfloat16
    pair, beta, gamma, y, z = where_am_i()
    k_irrep = pick(occ_irrep, window_k)
    pair_sym = pick(occ_irrep, pair_i) ^ pick(occ_irrep, pair_j)
    alpha = pair_sym[None, :] ^ k_irrep[:, None] ^ beta ^ gamma
    index = jnp.concatenate([(beta ^ pair_sym)[:, None], alpha.T], axis=1)
    blocks = jnp.take_along_axis(amplitudes, index[:, :, None], axis=1).reshape(PER, 1 + NW, BLK, BLK)
    send = blocks[:, 0].swapaxes(1, 2).reshape(PER, YS, BCH * BLK)
    tags = jnp.stack([pair_i, pair_j], axis=1).astype(half)[:, None, :]
    tail = jnp.pad(jnp.broadcast_to(tags, (PER, YS, 2)), ((0, 0), (0, 0), (0, CHL - BCH * BLK - 2)))
    hole = jnp.concatenate([send, tail], axis=2).swapaxes(0, 1).reshape(YS, PER * 16, 128)
    part = blocks[:, 1:].transpose(2, 1, 0, 3).reshape(BLK, NW * PER * BLK)
    part = jnp.pad(part, ((0, 0), (0, PACK - NW * PER * BLK)))

    columns = jnp.broadcast_to(vir_energy[:, :, None], (8, BLK, 128))
    rows = jnp.pad(vir_energy, ((0, 0), (0, 128 - BLK)), constant_values=20.0)[:, None, :]
    keep = occ_irrep[None, :, None] ^ gamma ^ occ_irrep[None, None, :] ^ k_irrep[:, None, None]
    coup = jnp.where((keep == 0)[..., None], couplings, jnp.zeros_like(couplings))
    coup = jnp.pad(coup, ((0, 0), (0, 0), (0, 2), (0, 128 - BLK))).transpose(1, 2, 0, 3).reshape(30, 32, 256)
    table = jnp.pad(jnp.stack([occ_irrep.astype(jnp.float32), occ_energy]), ((0, 6), (0, 98)))
    result = call(
        owner, occ_irrep, occ_energy, window_k, vir_energy,
        slabs.reshape(BLK, BLK * BLK), part, hole, coup, columns, rows, table)
    result = lax.dynamic_slice_in_dim(result, 4 * gamma, BLK // 2, 0)[:, :PER * BLK]
    return result.reshape(BLK // 2, PER, BLK).swapaxes(0, 1).reshape(PER, 1, BLK * BLK // 2)


def solution(mesh):
    placed = (
        P("pair", None, None),
        P("pair", "vtile", "irrep", None, None),
        P(None, None, None, "irrep"),
        P(),
        P(),
        P(),
        P("pair"),
        P("pair"),
        P(),
        P(),
    )
    return jax.shard_map(
        on_device,
        mesh=mesh,
        in_specs=placed,
        out_specs=P("pair", "vtile", "irrep"),
        check_vma=False,
    )
```

```python
import jax
import jax.numpy as jnp
from jax import lax
from jax.experimental import pallas as pl
from jax.experimental.pallas import tpu as pltpu
from jax.sharding import PartitionSpec as P

MESH = pl.DeviceIdType.MESH
YS, ZS, XS = 4, 8, 4
BLK = 88
PER = 5
NW = 2
BCH = BLK // YS
CHL = 2048
TILES = 16
ALL = 61
YPER = 2
YN = TILES // YPER
SKEW = 4
RING = 4
WEIGHTS = RING * 4 + 5
HOLES = WEIGHTS + 4
RIGHT, LEFT = 4, 3
PACK = 896
OUTL = 512
VM = pl.BlockSpec(memory_space=pltpu.VMEM)
SM = pl.BlockSpec(memory_space=pltpu.SMEM)


def where_am_i():
    pair, vtile, irrep = lax.axis_index("pair"), lax.axis_index("vtile"), lax.axis_index("irrep")
    return pair, vtile, irrep, lax.rem(pair, YS), pair // YS


def window_of(offset, width):
    base = offset // 128 * 128
    return base, 128 if offset - base + width <= 128 else 256


def cut(value, offset):
    moved = pltpu.roll(value, value.shape[1] - offset, 1) if offset else value
    moved = moved[:, :128]
    lane = lax.broadcasted_iota(jnp.int32, moved.shape, 1)
    return jnp.where(lane < BLK, moved, 0.0)


def kernel(
    owner_ref, irrep_ref, occ_ref, window_ref, vir_ref,
    slab_ref, part_ref, hole_ref, coup_ref, virs_ref,
    out_ref,
    tiles, ybuf, frecv, brecv, fsend, bsend, pall_ref, hall_ref,
    own, ystage, alphas, bases, column_ref, square, table_ref,
    wide, left, vshift, vt, vback, amp, weight, holes, column, acc,
    part0, part1, trip0, trip1, contrib,
    rbuf, slots, cbuf, merged, xbuf, total, zbuf,
    ys_sem, yr_sem, hs_sem, hr_sem, ps_sem, pr_sem,
    fs_sem, fr_sem, bs_sem, br_sem, zs_sem, zr_sem, local_sem,
    rs_sem, rr_sem, cs_sem, cr_sem, xs_sem, xr_sem, ts_sem, tr_sem,
):
    half, single = jnp.bfloat16, jnp.float32
    pair, vtile, irrep, y, z = where_am_i()
    x, core = vtile // 2, lax.rem(vtile, 2)
    zg = irrep * ZS + z

    def at_y(k):
        ty = lax.rem(y + k + YS, YS)
        return ty, (z * YS + ty, vtile, irrep)

    def at_z(step):
        tz = lax.rem(zg + step + 2 * ZS, 2 * ZS)
        return (lax.rem(tz, ZS) * YS + y, vtile, tz // ZS)

    def at_x(k):
        tx = lax.rem(x + k, XS)
        return tx, (pair, tx * 2 + core, irrep)

    at_core = (pair, x * 2 + 1 - core, irrep)
    at_irrep = (pair, vtile, 1 - irrep)
    barrier = pltpu.get_barrier_semaphore()
    for k in (1, 2, 3):
        pl.semaphore_signal(barrier, inc=1, device_id=at_y(k)[1], device_id_type=MESH)
        pl.semaphore_signal(barrier, inc=1, device_id=at_x(k)[1], device_id_type=MESH)
    pl.semaphore_signal(barrier, inc=1, device_id=at_core, device_id_type=MESH)
    pl.semaphore_signal(barrier, inc=1, device_id=at_irrep, device_id_type=MESH)
    for step in (1, -1):
        pl.semaphore_signal(barrier, inc=1, device_id=at_z(step), device_id_type=MESH)
    for t in range(ALL - 1):
        tiles[t] = slab_ref[:, 128 * t:128 * t + 128]
    tiles[ALL - 1] = jnp.zeros((BLK, 128), jnp.bfloat16)
    tiles[ALL - 1, :, :64] = slab_ref[:, 128 * (ALL - 1):]
    square[...] = jnp.zeros((128, 128), single)
    square[:8, :BLK] = virs_ref[...]
    upright = square[...].T
    for h in range(8):
        column_ref[h] = jnp.broadcast_to(upright[:BLK, h:h + 1], (BLK, 128))
    lane_of = lax.broadcasted_iota(jnp.int32, (1, 128), 1)
    irreps, energies = jnp.zeros((1, 128), jnp.int32), jnp.zeros((1, 128), single)
    for l in range(30):
        irreps = jnp.where(lane_of == l, irrep_ref[l], irreps)
        energies = jnp.where(lane_of == l, occ_ref[l], energies)
    table_ref[0:1, :] = irreps.astype(single)
    table_ref[1:2, :] = energies
    ystage[...] = jnp.zeros((NW, 24 * 32, 128), single)
    pl.semaphore_wait(barrier, 10)

    def hole_copy(k):
        ty, target = at_y(k)
        return pltpu.make_async_remote_copy(
            src_ref=hole_ref.at[ty], dst_ref=hall_ref.at[z, y],
            send_sem=hs_sem.at[k - 1], recv_sem=hr_sem.at[k - 1],
            device_id=target, device_id_type=MESH)

    def part_copy(k):
        _, target = at_y(k)
        return pltpu.make_async_remote_copy(
            src_ref=part_ref, dst_ref=pall_ref.at[y],
            send_sem=ps_sem.at[k - 1], recv_sem=pr_sem.at[k - 1],
            device_id=target, device_id_type=MESH)

    def slab_copy(k, n):
        ty, target = at_y(k)
        return pltpu.make_async_remote_copy(
            src_ref=tiles.at[pl.ds(ty * 15 + n * YPER, YPER)],
            dst_ref=ybuf.at[y, pl.ds(n * YPER, YPER)],
            send_sem=ys_sem.at[k - 1, n], recv_sem=yr_sem.at[k - 1, n],
            device_id=target, device_id_type=MESH)

    def ring_copy(index):
        step = index if index < RIGHT else index - RIGHT
        right = index < RIGHT
        held = lax.rem(zg + (-step if right else step) + 2 * ZS, ZS)
        return pltpu.make_async_remote_copy(
            src_ref=hall_ref.at[held], dst_ref=hall_ref.at[held],
            send_sem=zs_sem.at[index], recv_sem=zr_sem.at[index],
            device_id=at_z(1 if right else -1), device_id_type=MESH)

    def chain_copy(forward, n):
        src, dst = (fsend, frecv) if forward else (bsend, brecv)
        send, recv = (fs_sem, fr_sem) if forward else (bs_sem, br_sem)
        tz = jnp.minimum(z + 1, ZS - 1) if forward else jnp.maximum(z - 1, 0)
        return pltpu.make_async_remote_copy(
            src_ref=src.at[n], dst_ref=dst.at[n],
            send_sem=send.at[n], recv_sem=recv.at[n],
            device_id=(tz * YS + y, vtile, irrep), device_id_type=MESH)

    for k in (1, 3, 2):
        hole_copy(k).start()

    def send_chunk(n, _):
        for k in (1, 3, 2):
            slab_copy(k, n).start()
        return 0

    lax.fori_loop(0, YN, send_chunk, 0)
    for k in (1, 3, 2):
        part_copy(k).start()

    own_slab = pltpu.make_async_copy(tiles.at[pl.ds(y * 15, TILES)], ybuf.at[y], local_sem.at[0])
    own_part = pltpu.make_async_copy(part_ref, pall_ref.at[y], local_sem.at[1])
    own_hole = pltpu.make_async_copy(hole_ref.at[y], hall_ref.at[z, y], local_sem.at[2])
    for copy in (own_hole, own_slab, own_part):
        copy.start()
    own_hole.wait()
    for k in (1, 2, 3):
        hole_copy(k).wait_recv()
    ring_copy(0).start()
    ring_copy(RIGHT).start()
    own_slab.wait()
    own_part.wait()

    mine_f = hall_ref[z].astype(single)
    for source in range(YS):
        own[80 * source:80 * source + 80, :] = mine_f[source]
    pairs = own[pl.ds(15, YS * PER, stride=16), :]
    lane20 = lax.broadcasted_iota(jnp.int32, (YS * PER, 128), 1).astype(single)
    is_first, is_second = pairs[:, 16:17] == lane20, pairs[:, 17:18] == lane20

    def look(mask, row):
        return jnp.sum(jnp.where(mask, table_ref[row:row + 1, :], 0.0), axis=1, keepdims=True)

    second_irrep = look(is_second, 0).astype(jnp.int32)
    sym = look(is_first, 0).astype(jnp.int32) ^ second_irrep
    energy2 = look(is_first, 1) + look(is_second, 1)
    for w in range(NW):
        shift = irrep_ref[window_ref[w]] ^ vtile ^ irrep
        alphas[w] = jnp.broadcast_to(sym ^ shift, (YS * PER, 128))
        bases[w] = jnp.broadcast_to(energy2 + occ_ref[window_ref[w]], (YS * PER, 128))
    choose = is_second.astype(single)[:, :30].astype(half)
    for w in range(NW):
        wanted = second_irrep ^ irrep_ref[window_ref[w]] ^ irrep
        for l in range(30):
            found = jnp.dot(choose, coup_ref[w, l], preferred_element_type=single)
            ystage[w, 24 * l:24 * l + YS * PER, :BLK] = jnp.where(wanted == irrep_ref[l], found, 0.0)

    root_y = [lax.rem(owner_ref[w], YS) for w in range(NW)]
    root_z = [owner_ref[w] // YS for w in range(NW)]

    def candidate(w, n):
        value = ybuf[0, n]
        for source in range(1, YS):
            value = jnp.where(root_y[w] == source, ybuf[source, n], value)
        return value

    def chain_event(forward, n):
        src, dst = (fsend, frecv) if forward else (bsend, brecv)
        first_here = z <= 3 if forward else z >= 4
        start, end = (z == 0, z == ZS - 1) if forward else (z == ZS - 1, z == 0)

        @pl.when(jnp.logical_and(first_here, lax.rem(n, YPER) == 0))
        def _():
            for k in (1, 2, 3):
                slab_copy(k, n // YPER).wait_recv()

        mine = [candidate(w, n) for w in range(NW)]

        @pl.when(start)
        def _():
            for w in range(NW):
                dst[n, w] = mine[w]

        @pl.when(jnp.logical_not(start))
        def _():
            chain_copy(forward, n).wait_recv()

        @pl.when(jnp.logical_not(end))
        def _():
            for w in range(NW):
                src[n, w] = jnp.where(root_z[w] == z, mine[w], dst[n, w])
            chain_copy(forward, n).start()

    def hole_unit(index, p, place):
        source = lax.rem(y + index + 1, YS)
        lanes = pl.ds(pl.multiple_of(p * 256, 256), 256)
        holes[place, :, lanes] = jnp.dot(
            left[:BCH * BLK, :], weight[source, :, lanes], preferred_element_type=single)

    def chain_step(t, _):
        nf = t - SKEW * z
        nb = t - SKEW * (ZS - 1 - z)

        @pl.when(jnp.logical_and(nf >= 0, nf < TILES))
        def _():
            chain_event(True, nf)

        @pl.when(jnp.logical_and(nb >= 0, nb < TILES))
        def _():
            chain_event(False, nb)

        for step in range(1, RIGHT):
            @pl.when(t == RING * step)
            def _():
                ring_copy(step - 1).wait_recv()
                ring_copy(step).start()
                if step < LEFT:
                    ring_copy(RIGHT + step - 1).wait_recv()
                    ring_copy(RIGHT + step).start()
        @pl.when(t == RING * RIGHT)
        def _():
            ring_copy(RIGHT - 1).wait_recv()
            ring_copy(RIGHT + LEFT - 1).wait_recv()
            for block in range(ZS * YS):
                wide[80 * block:80 * block + 80, :] = hall_ref[block // YS, block % YS].astype(single)

        for quarter in range(4):
            @pl.when(t == RING * RIGHT + 1 + quarter)
            def _():
                for k in range(4 * quarter, 4 * quarter + 4):
                    tile = wide[pl.ds(k, 160, stride=16), :]
                    left[128 * k:128 * k + 128, :] = tile.T.astype(half)

        @pl.when(jnp.logical_and(t >= WEIGHTS, t < WEIGHTS + YS))
        def _():
            source = t - WEIGHTS
            table = wide[pl.ds(15, 160, stride=16), :]
            slot = lax.broadcasted_iota(jnp.int32, (160, 32), 1).astype(single)
            member = table[:, 17:18] == slot
            for p in range(PER):
                row = own[pl.ds(80 * source + 16 * p + 15, 1), :]
                here = jnp.logical_and(member, table[:, 16:17] == row[:, 16:17])
                rows = jnp.concatenate(
                    [ystage[w, pl.ds(source * PER + p, 32, stride=24), :] for w in range(NW)], axis=1)
                weight[source, :, 256 * p:256 * p + 256] = jnp.dot(
                    here.astype(single).astype(half), rows.astype(half), preferred_element_type=single).astype(half)

        @pl.when(jnp.logical_and(t >= HOLES, t < HOLES + 3 * PER))
        def _():
            hole_unit((t - HOLES) // PER, lax.rem(t - HOLES, PER), (t - HOLES) // PER)

        return 0

    lax.fori_loop(0, TILES + SKEW * (ZS - 1), chain_step, 0)

    for k in (1, 2, 3):
        part_copy(k).wait_recv()
    for w in range(NW):
        for t in range(TILES):
            other = jnp.where(root_z[w] < z, frecv[t, w], brecv[t, w])
            vshift[:, 128 * t:128 * t + 128] = jnp.where(
                root_z[w] == z, candidate(w, t), other).astype(single)
        for shift in range(1, YS):
            @pl.when(y == shift)
            def _():
                if shift:
                    vshift[...] = pltpu.roll(vshift[...], CHL - 16 * shift, 1)
        for b in range(BCH):
            base, width = window_of(BLK * b, BLK)
            tile = cut(vshift[:, base:base + width], BLK * b - base)
            vt[w, :, 128 * b:128 * b + 128] = tile.astype(half)
            vback[w, 128 * b:128 * b + 128, :BLK] = tile.T.astype(half)
        for source in range(YS):
            parts = []
            for p in range(PER):
                offset = BLK * (w * PER + p)
                base, width = window_of(offset, BLK)
                parts.append(cut(pall_ref[source, :, base:base + width].astype(single), offset - base))
            amp[w, source] = jnp.concatenate(parts, axis=0).astype(half)
    vback[:, :, BLK:] = jnp.zeros((NW, 128 * BCH, 128 - BLK), half)
    contrib[:, :, 880:PACK] = jnp.zeros((YS, BLK, PACK - 880), single)
    def ycopy(k):
        ty, target = at_y(k)
        return pltpu.make_async_remote_copy(
            src_ref=contrib.at[ty], dst_ref=rbuf.at[k - 1],
            send_sem=rs_sem.at[k - 1], recv_sem=rr_sem.at[k - 1],
            device_id=target, device_id_type=MESH)

    gamma_row = square[pl.ds(irrep, 1), :]
    gamma_row = jnp.where(lax.broadcasted_iota(jnp.int32, (1, 128), 1) < BLK, gamma_row, 20.0)

    def source_step(index, _):
        source = lax.rem(y + index + 1, YS)

        place = lax.rem(index, 3)

        @pl.when(index == YS - 1)
        def _():
            def hole_step(p, _):
                hole_unit(YS - 1, p, 0)
                return 0

            lax.fori_loop(0, PER, hole_step, 0)

        for w in range(NW):
            for p in range(PER):
                here = pl.ds(source * PER + p, 1)
                alpha, energy = alphas[w, here, :], column_ref[0]
                for h in range(1, 8):
                    energy = jnp.where(alpha == h, column_ref[h], energy)
                column[BLK * p:BLK * p + BLK, :] = energy - bases[w, here, :]

            def lanes_of(t):
                return pl.ds(pl.multiple_of(t * 256, 256), 256)

            def particle(t):
                return jnp.dot(amp[w, source, :, :BLK], vt[w, :, lanes_of(t)], preferred_element_type=single)

            def stage(t, now, later, fill, drain):
                if later is not None:
                    later[...] = particle(t + 1)
                acc[...] += jnp.dot(
                    drain[...], vback[w, lanes_of(jnp.maximum(t - 1, 0)), :], preferred_element_type=single)
                for side in range(2):
                    b = 2 * t + side
                    rows = pl.ds(pl.multiple_of(b * BLK, 8), BLK)
                    hole = jnp.concatenate([
                        holes[place, rows, 256 * p + 128 * w:256 * p + 128 * w + 128] for p in range(PER)], axis=0)
                    energy = gamma_row + vir_ref[vtile, y * BCH + b]
                    inverse = pltpu.reciprocal(column[...] + energy, approx=True)
                    fill[:, 128 * side:128 * side + 128] = (
                        (now[:, 128 * side:128 * side + 128] - hole) * inverse).astype(half)

            acc[...] = jnp.zeros_like(acc)
            trip1[...] = jnp.zeros_like(trip1)
            part0[...] = particle(0)

            def two_steps(u, _):
                stage(2 * u, part0, part1, trip0, trip1)
                stage(2 * u + 1, part1, part0, trip1, trip0)
                return 0

            lax.fori_loop(0, BCH // 4, two_steps, 0)
            stage(BCH // 2 - 1, part0, None, trip0, trip1)
            acc[...] += jnp.dot(trip0[...], vback[w, 128 * (BCH - 2):, :], preferred_element_type=single)
            for p in range(PER):
                offset = BLK * (w * PER + p)
                contrib[source, :, offset:offset + BLK] = acc[BLK * p:BLK * p + BLK, :BLK]

        @pl.when(index < YS - 1)
        def _():
            ty, target = at_y(index + 1)
            pltpu.make_async_remote_copy(
                src_ref=contrib.at[ty], dst_ref=rbuf.at[index],
                send_sem=rs_sem.at[index], recv_sem=rr_sem.at[index],
                device_id=target, device_id_type=MESH).start()

        return 0

    lax.fori_loop(0, YS, source_step, 0)
    for k in (1, 2, 3):
        ycopy(k).wait()
    summed = contrib[y] + rbuf[0] + rbuf[1] + rbuf[2]
    windows = [summed[:, :OUTL], pltpu.roll(summed, PACK - 440, 1)[:, :OUTL]]
    lane = lax.broadcasted_iota(jnp.int32, (1, OUTL), 1)
    codes = []
    for w in range(NW):
        code = jnp.full((1, OUTL), -1, jnp.int32)
        for p in range(PER):
            inside = jnp.logical_and(lane >= BLK * p, lane < BLK * (p + 1))
            alpha = jnp.concatenate([alphas[w, pl.ds(y * PER + p, 1), :]] * 4, axis=1)
            code = jnp.where(inside, alpha, code)
        codes.append(code)
    ccopies, xcopies, zcopies = [], [], []
    for part in range(2):
        lanes = slice(256 * part, 256 * part + 256)
        for target in range(2 * XS):
            slots[part, target % 2, target // 2] = sum(
                jnp.where(codes[w][:, lanes] == target, windows[w][:, lanes], 0.0) for w in range(NW))
        ccopies.append(pltpu.make_async_remote_copy(
            src_ref=slots.at[part, 1 - core], dst_ref=cbuf.at[part],
            send_sem=cs_sem.at[part], recv_sem=cr_sem.at[part], device_id=at_core, device_id_type=MESH))
        ccopies[part].start()
    for part in range(2):
        ccopies[part].wait()
        for tx in range(XS):
            merged[part, tx] = slots[part, core, tx] + cbuf[part, tx]
        sends = []
        for k in (1, 3, 2):
            tx, target = at_x(k)
            sends.append(pltpu.make_async_remote_copy(
                src_ref=merged.at[part, tx], dst_ref=xbuf.at[part, k - 1],
                send_sem=xs_sem.at[part, k - 1], recv_sem=xr_sem.at[part, k - 1],
                device_id=target, device_id_type=MESH))
        for copy in sends:
            copy.start()
        xcopies.append(sends)
    for part in range(2):
        for copy in xcopies[part]:
            copy.wait()
        total[part] = merged[part, x] + xbuf[part, 0] + xbuf[part, 1] + xbuf[part, 2]
        zcopies.append(pltpu.make_async_remote_copy(
            src_ref=total.at[part, pl.ds(pl.multiple_of(40 * (1 - irrep), 8), 48), :], dst_ref=zbuf.at[part],
            send_sem=ts_sem.at[part], recv_sem=tr_sem.at[part], device_id=at_irrep, device_id_type=MESH))
        zcopies[part].start()
    def sent(n, _):
        @pl.when(z < ZS - 1)
        def _():
            chain_copy(True, n).wait_send()

        @pl.when(z > 0)
        def _():
            chain_copy(False, n).wait_send()

        return 0

    lax.fori_loop(0, TILES, sent, 0)

    def sent_y(n, _):
        for k in (1, 2, 3):
            slab_copy(k, n).wait_send()
        return 0

    lax.fori_loop(0, YN, sent_y, 0)
    for k in (1, 2, 3):
        hole_copy(k).wait_send()
        part_copy(k).wait_send()
    for index in range(RIGHT + LEFT):
        ring_copy(index).wait_send()
    for part in range(2):
        zcopies[part].wait()
        out_ref[:, 256 * part:256 * part + 256] = (
            total[part, pl.ds(pl.multiple_of(40 * irrep, 8), 48), :] + zbuf[part])


DMA = pltpu.SemaphoreType.DMA


def call(*operands):
    half, single = jnp.bfloat16, jnp.float32
    return pl.pallas_call(
        kernel,
        out_shape=jax.ShapeDtypeStruct((48, OUTL), single),
        in_specs=[SM] * 5 + [VM] * 5,
        out_specs=VM,
        scratch_shapes=[
            pltpu.VMEM((ALL, BLK, 128), half),
            pltpu.VMEM((YS, TILES, BLK, 128), half),
            pltpu.VMEM((TILES, NW, BLK, 128), half),
            pltpu.VMEM((TILES, NW, BLK, 128), half),
            pltpu.VMEM((TILES, NW, BLK, 128), half),
            pltpu.VMEM((TILES, NW, BLK, 128), half),
            pltpu.VMEM((YS, BLK, PACK), half),
            pltpu.VMEM((ZS, YS, 80, 128), half),
            pltpu.VMEM((YS * 80, 128), single),
            pltpu.VMEM((NW, 24 * 32, 128), single),
            pltpu.VMEM((NW, YS * PER, 128), jnp.int32),
            pltpu.VMEM((NW, YS * PER, 128), single),
            pltpu.VMEM((8, BLK, 128), single),
            pltpu.VMEM((128, 128), single),
            pltpu.VMEM((8, 128), single),
            pltpu.VMEM((2560, 128), single),
            pltpu.VMEM((CHL, 160), half),
            pltpu.VMEM((BLK, CHL), single),
            pltpu.VMEM((NW, BLK, 128 * BCH), half),
            pltpu.VMEM((NW, 128 * BCH, 128), half),
            pltpu.VMEM((NW, YS, PER * BLK, 128), half),
            pltpu.VMEM((YS, 160, 256 * PER), half),
            pltpu.VMEM((3, BCH * BLK, 256 * PER), single),
            pltpu.VMEM((PER * BLK, 128), single),
            pltpu.VMEM((PER * BLK, 128), single),
            pltpu.VMEM((PER * BLK, 256), single),
            pltpu.VMEM((PER * BLK, 256), single),
            pltpu.VMEM((PER * BLK, 256), half),
            pltpu.VMEM((PER * BLK, 256), half),
            pltpu.VMEM((YS, BLK, PACK), single),
            pltpu.VMEM((3, BLK, PACK), single),
            pltpu.VMEM((2, 2, XS, BLK, 256), single),
            pltpu.VMEM((2, XS, BLK, 256), single),
            pltpu.VMEM((2, XS, BLK, 256), single),
            pltpu.VMEM((2, 3, BLK, 256), single),
            pltpu.VMEM((2, BLK, 256), single),
            pltpu.VMEM((2, 48, 256), single),
            DMA((3, YN)), DMA((3, YN)), DMA((3,)), DMA((3,)), DMA((3,)), DMA((3,)),
            DMA((TILES,)), DMA((TILES,)), DMA((TILES,)), DMA((TILES,)), DMA((7,)), DMA((7,)), DMA((3,)),
            DMA((3,)), DMA((3,)), DMA((2,)), DMA((2,)), DMA((2, 3)), DMA((2, 3)), DMA((2,)), DMA((2,)),
        ],
        compiler_params=pltpu.CompilerParams(
            collective_id=0, has_side_effects=True, vmem_limit_bytes=62 * 2**20),
    )(*operands)


def pick(table, index):
    places = jnp.arange(table.shape[0], dtype=jnp.int32)
    return jnp.sum(jnp.where(index[..., None] == places, table, 0), axis=-1)


def on_device(
    amplitudes, slabs, couplings, occ_energy, vir_energy, occ_irrep, pair_i, pair_j, window_k, owner
):
    half = jnp.bfloat16
    pair, beta, gamma, y, z = where_am_i()
    k_irrep = pick(occ_irrep, window_k)
    pair_sym = pick(occ_irrep, pair_i) ^ pick(occ_irrep, pair_j)
    alpha = pair_sym[None, :] ^ k_irrep[:, None] ^ beta ^ gamma
    index = jnp.concatenate([(beta ^ pair_sym)[:, None], alpha.T], axis=1)
    blocks = jnp.take_along_axis(amplitudes, index[:, :, None], axis=1).reshape(PER, 1 + NW, BLK, BLK)
    send = blocks[:, 0].swapaxes(1, 2).reshape(PER, YS, BCH * BLK)
    tags = jnp.stack([pair_i, pair_j], axis=1).astype(half)[:, None, :]
    tail = jnp.pad(jnp.broadcast_to(tags, (PER, YS, 2)), ((0, 0), (0, 0), (0, CHL - BCH * BLK - 2)))
    hole = jnp.concatenate([send, tail], axis=2).swapaxes(0, 1).reshape(YS, PER * 16, 128)
    part = blocks[:, 1:].transpose(2, 1, 0, 3).reshape(BLK, NW * PER * BLK)
    part = jnp.pad(part, ((0, 0), (0, PACK - NW * PER * BLK)))

    result = call(
        owner, occ_irrep, occ_energy, window_k, vir_energy,
        slabs.reshape(BLK, BLK * BLK), part, hole, couplings, vir_energy)
    result = lax.dynamic_slice_in_dim(result, 4 * gamma, BLK // 2, 0)[:, :PER * BLK]
    return result.reshape(BLK // 2, PER, BLK).swapaxes(0, 1).reshape(PER, 1, BLK * BLK // 2)


def solution(mesh):
    placed = (
        P("pair", None, None),
        P("pair", "vtile", "irrep", None, None),
        P(None, None, None, "irrep"),
        P(),
        P(),
        P(),
        P("pair"),
        P("pair"),
        P(),
        P(),
    )
    return jax.shard_map(
        on_device,
        mesh=mesh,
        in_specs=placed,
        out_specs=P("pair", "vtile", "irrep"),
        check_vma=False,
    )
```

```python
import jax
import jax.numpy as jnp
from jax import lax
from jax.experimental import pallas as pl
from jax.experimental.pallas import tpu as pltpu
from jax.sharding import PartitionSpec as P

MESH = pl.DeviceIdType.MESH
YS, ZS, XS = 4, 8, 4
BLK = 88
PER = 5
NW = 2
BCH = BLK // YS
CHL = 2048
TILES = 16
ALL = 61
YPER = 2
YN = TILES // YPER
SKEW = 4
RING = 4
UNITS = 24
RIGHT, LEFT = 4, 3
PACK = 896
OUTL = 512
VM = pl.BlockSpec(memory_space=pltpu.VMEM)
SM = pl.BlockSpec(memory_space=pltpu.SMEM)


def where_am_i():
    pair, vtile, irrep = lax.axis_index("pair"), lax.axis_index("vtile"), lax.axis_index("irrep")
    return pair, vtile, irrep, lax.rem(pair, YS), pair // YS


def window_of(offset, width):
    base = offset // 128 * 128
    return base, 128 if offset - base + width <= 128 else 256


def cut(value, offset):
    moved = pltpu.roll(value, value.shape[1] - offset, 1) if offset else value
    moved = moved[:, :128]
    lane = lax.broadcasted_iota(jnp.int32, moved.shape, 1)
    return jnp.where(lane < BLK, moved, 0.0)


def kernel(
    owner_ref, irrep_ref, occ_ref, window_ref, vir_ref,
    slab_ref, part_ref, hole_ref, coup_ref, virs_ref,
    out_ref,
    tiles, ybuf, frecv, brecv, fsend, bsend, pall_ref, hall_ref,
    own, ystage, alphas, bases, column_ref, square, table_ref,
    wide, left, vshift, vt, vback, amp, weight, holes, column, acc,
    part0, part1, trip0, trip1, contrib,
    rbuf, slots, cbuf, merged, xbuf, total, zbuf,
    ys_sem, yr_sem, hs_sem, hr_sem, ps_sem, pr_sem,
    fs_sem, fr_sem, bs_sem, br_sem, zs_sem, zr_sem, local_sem,
    rs_sem, rr_sem, cs_sem, cr_sem, xs_sem, xr_sem, ts_sem, tr_sem,
):
    half, single = jnp.bfloat16, jnp.float32
    pair, vtile, irrep, y, z = where_am_i()
    x, core = vtile // 2, lax.rem(vtile, 2)
    zg = irrep * ZS + z

    def at_y(k):
        ty = lax.rem(y + k + YS, YS)
        return ty, (z * YS + ty, vtile, irrep)

    def at_z(step):
        tz = lax.rem(zg + step + 2 * ZS, 2 * ZS)
        return (lax.rem(tz, ZS) * YS + y, vtile, tz // ZS)

    def at_x(k):
        tx = lax.rem(x + k, XS)
        return tx, (pair, tx * 2 + core, irrep)

    at_core = (pair, x * 2 + 1 - core, irrep)
    at_irrep = (pair, vtile, 1 - irrep)
    barrier = pltpu.get_barrier_semaphore()
    for k in (1, 2, 3):
        pl.semaphore_signal(barrier, inc=1, device_id=at_y(k)[1], device_id_type=MESH)
        pl.semaphore_signal(barrier, inc=1, device_id=at_x(k)[1], device_id_type=MESH)
    pl.semaphore_signal(barrier, inc=1, device_id=at_core, device_id_type=MESH)
    pl.semaphore_signal(barrier, inc=1, device_id=at_irrep, device_id_type=MESH)
    for step in (1, -1):
        pl.semaphore_signal(barrier, inc=1, device_id=at_z(step), device_id_type=MESH)
    for t in range(ALL - 1):
        tiles[t] = slab_ref[:, 128 * t:128 * t + 128]
    tiles[ALL - 1] = jnp.zeros((BLK, 128), jnp.bfloat16)
    tiles[ALL - 1, :, :64] = slab_ref[:, 128 * (ALL - 1):]
    square[...] = jnp.zeros((128, 128), single)
    square[:8, :BLK] = virs_ref[...]
    upright = square[...].T
    for h in range(8):
        column_ref[h] = jnp.broadcast_to(upright[:BLK, h:h + 1], (BLK, 128))
    lane_of = lax.broadcasted_iota(jnp.int32, (1, 128), 1)
    irreps, energies = jnp.zeros((1, 128), jnp.int32), jnp.zeros((1, 128), single)
    for l in range(30):
        irreps = jnp.where(lane_of == l, irrep_ref[l], irreps)
        energies = jnp.where(lane_of == l, occ_ref[l], energies)
    table_ref[0:1, :] = irreps.astype(single)
    table_ref[1:2, :] = energies
    ystage[...] = jnp.zeros((NW, 24 * 32, 128), single)
    pl.semaphore_wait(barrier, 10)

    def hole_copy(k):
        ty, target = at_y(k)
        return pltpu.make_async_remote_copy(
            src_ref=hole_ref.at[ty], dst_ref=hall_ref.at[z, y],
            send_sem=hs_sem.at[k - 1], recv_sem=hr_sem.at[k - 1],
            device_id=target, device_id_type=MESH)

    def part_copy(k):
        _, target = at_y(k)
        return pltpu.make_async_remote_copy(
            src_ref=part_ref, dst_ref=pall_ref.at[y],
            send_sem=ps_sem.at[k - 1], recv_sem=pr_sem.at[k - 1],
            device_id=target, device_id_type=MESH)

    def slab_copy(k, n):
        ty, target = at_y(k)
        return pltpu.make_async_remote_copy(
            src_ref=tiles.at[pl.ds(ty * 15 + n * YPER, YPER)],
            dst_ref=ybuf.at[y, pl.ds(n * YPER, YPER)],
            send_sem=ys_sem.at[k - 1, n], recv_sem=yr_sem.at[k - 1, n],
            device_id=target, device_id_type=MESH)

    def ring_copy(index):
        step = index if index < RIGHT else index - RIGHT
        right = index < RIGHT
        held = lax.rem(zg + (-step if right else step) + 2 * ZS, ZS)
        return pltpu.make_async_remote_copy(
            src_ref=hall_ref.at[held], dst_ref=hall_ref.at[held],
            send_sem=zs_sem.at[index], recv_sem=zr_sem.at[index],
            device_id=at_z(1 if right else -1), device_id_type=MESH)

    def chain_copy(forward, n):
        src, dst = (fsend, frecv) if forward else (bsend, brecv)
        send, recv = (fs_sem, fr_sem) if forward else (bs_sem, br_sem)
        tz = jnp.minimum(z + 1, ZS - 1) if forward else jnp.maximum(z - 1, 0)
        return pltpu.make_async_remote_copy(
            src_ref=src.at[n], dst_ref=dst.at[n],
            send_sem=send.at[n], recv_sem=recv.at[n],
            device_id=(tz * YS + y, vtile, irrep), device_id_type=MESH)

    for k in (1, 3, 2):
        hole_copy(k).start()

    def send_chunk(n, _):
        for k in (1, 3, 2):
            slab_copy(k, n).start()
        return 0

    lax.fori_loop(0, YN, send_chunk, 0)
    for k in (1, 3, 2):
        part_copy(k).start()

    own_slab = pltpu.make_async_copy(tiles.at[pl.ds(y * 15, TILES)], ybuf.at[y], local_sem.at[0])
    own_part = pltpu.make_async_copy(part_ref, pall_ref.at[y], local_sem.at[1])
    own_hole = pltpu.make_async_copy(hole_ref.at[y], hall_ref.at[z, y], local_sem.at[2])
    for copy in (own_hole, own_slab, own_part):
        copy.start()
    own_hole.wait()
    for k in (1, 2, 3):
        hole_copy(k).wait_recv()
    ring_copy(0).start()
    ring_copy(RIGHT).start()
    own_slab.wait()
    own_part.wait()

    mine_f = hall_ref[z].astype(single)
    for source in range(YS):
        own[80 * source:80 * source + 80, :] = mine_f[source]
    pairs = own[pl.ds(15, YS * PER, stride=16), :]
    lane20 = lax.broadcasted_iota(jnp.int32, (YS * PER, 128), 1).astype(single)
    is_first, is_second = pairs[:, 16:17] == lane20, pairs[:, 17:18] == lane20

    def look(mask, row):
        return jnp.sum(jnp.where(mask, table_ref[row:row + 1, :], 0.0), axis=1, keepdims=True)

    second_irrep = look(is_second, 0).astype(jnp.int32)
    sym = look(is_first, 0).astype(jnp.int32) ^ second_irrep
    energy2 = look(is_first, 1) + look(is_second, 1)
    for w in range(NW):
        shift = irrep_ref[window_ref[w]] ^ vtile ^ irrep
        alphas[w] = jnp.broadcast_to(sym ^ shift, (YS * PER, 128))
        bases[w] = jnp.broadcast_to(energy2 + occ_ref[window_ref[w]], (YS * PER, 128))
    choose = is_second.astype(single)[:, :30].astype(half)
    for w in range(NW):
        wanted = second_irrep ^ irrep_ref[window_ref[w]] ^ irrep
        for l in range(30):
            found = jnp.dot(choose, coup_ref[w, l], preferred_element_type=single)
            ystage[w, 24 * l:24 * l + YS * PER, :BLK] = jnp.where(wanted == irrep_ref[l], found, 0.0)

    root_y = [lax.rem(owner_ref[w], YS) for w in range(NW)]
    root_z = [owner_ref[w] // YS for w in range(NW)]

    def candidate(w, n):
        value = ybuf[0, n]
        for source in range(1, YS):
            value = jnp.where(root_y[w] == source, ybuf[source, n], value)
        return value

    def chain_event(forward, n):
        src, dst = (fsend, frecv) if forward else (bsend, brecv)
        first_here = z <= 3 if forward else z >= 4
        start, end = (z == 0, z == ZS - 1) if forward else (z == ZS - 1, z == 0)

        @pl.when(jnp.logical_and(first_here, lax.rem(n, YPER) == 0))
        def _():
            for k in (1, 2, 3):
                slab_copy(k, n // YPER).wait_recv()

        mine = [candidate(w, n) for w in range(NW)]

        @pl.when(start)
        def _():
            for w in range(NW):
                dst[n, w] = mine[w]

        @pl.when(jnp.logical_not(start))
        def _():
            chain_copy(forward, n).wait_recv()

        @pl.when(jnp.logical_not(end))
        def _():
            for w in range(NW):
                src[n, w] = jnp.where(root_z[w] == z, mine[w], dst[n, w])
            chain_copy(forward, n).start()

    def hole_unit(index, p, place):
        source = lax.rem(y + index + 1, YS)
        lanes = pl.ds(pl.multiple_of(p * 256, 256), 256)
        holes[place, :, lanes] = jnp.dot(
            left[:BCH * BLK, :], weight[source, :, lanes], preferred_element_type=single)

    begin = RING * RIGHT + 5 * jnp.minimum(z, ZS - 1 - z)

    def chain_step(t, _):
        nf = t - SKEW * z
        nb = t - SKEW * (ZS - 1 - z)

        @pl.when(jnp.logical_and(nf >= 0, nf < TILES))
        def _():
            chain_event(True, nf)

        @pl.when(jnp.logical_and(nb >= 0, nb < TILES))
        def _():
            chain_event(False, nb)

        for step in range(1, RIGHT):
            @pl.when(t == RING * step)
            def _():
                ring_copy(step - 1).wait_recv()
                ring_copy(step).start()
                if step < LEFT:
                    ring_copy(RIGHT + step - 1).wait_recv()
                    ring_copy(RIGHT + step).start()
        @pl.when(t == begin)
        def _():
            ring_copy(RIGHT - 1).wait_recv()
            ring_copy(RIGHT + LEFT - 1).wait_recv()
            for block in range(ZS * YS):
                wide[80 * block:80 * block + 80, :] = hall_ref[block // YS, block % YS].astype(single)

        for quarter in range(4):
            @pl.when(t == begin + 1 + quarter)
            def _():
                for k in range(4 * quarter, 4 * quarter + 4):
                    tile = wide[pl.ds(k, 160, stride=16), :]
                    left[128 * k:128 * k + 128, :] = tile.T.astype(half)

        @pl.when(jnp.logical_and(t >= (begin + 5), t < (begin + 5) + YS))
        def _():
            source = t - (begin + 5)
            table = wide[pl.ds(15, 160, stride=16), :]
            slot = lax.broadcasted_iota(jnp.int32, (160, 32), 1).astype(single)
            member = table[:, 17:18] == slot
            for p in range(PER):
                row = own[pl.ds(80 * source + 16 * p + 15, 1), :]
                here = jnp.logical_and(member, table[:, 16:17] == row[:, 16:17])
                rows = jnp.concatenate(
                    [ystage[w, pl.ds(source * PER + p, 32, stride=24), :] for w in range(NW)], axis=1)
                weight[source, :, 256 * p:256 * p + 256] = jnp.dot(
                    here.astype(single).astype(half), rows.astype(half), preferred_element_type=single).astype(half)

        @pl.when(jnp.logical_and(t >= (begin + 9), t < (begin + 9) + 3 * PER))
        def _():
            hole_unit((t - (begin + 9)) // PER, lax.rem(t - (begin + 9), PER), (t - (begin + 9)) // PER)

        return 0

    lax.fori_loop(0, RING * RIGHT + 15 + UNITS + 1, chain_step, 0)

    for k in (1, 2, 3):
        part_copy(k).wait_recv()
    for w in range(NW):
        for t in range(TILES):
            other = jnp.where(root_z[w] < z, frecv[t, w], brecv[t, w])
            vshift[:, 128 * t:128 * t + 128] = jnp.where(
                root_z[w] == z, candidate(w, t), other).astype(single)
        for shift in range(1, YS):
            @pl.when(y == shift)
            def _():
                if shift:
                    vshift[...] = pltpu.roll(vshift[...], CHL - 16 * shift, 1)
        for b in range(BCH):
            base, width = window_of(BLK * b, BLK)
            tile = cut(vshift[:, base:base + width], BLK * b - base)
            vt[w, :, 128 * b:128 * b + 128] = tile.astype(half)
            vback[w, 128 * b:128 * b + 128, :BLK] = tile.T.astype(half)
        for source in range(YS):
            parts = []
            for p in range(PER):
                offset = BLK * (w * PER + p)
                base, width = window_of(offset, BLK)
                parts.append(cut(pall_ref[source, :, base:base + width].astype(single), offset - base))
            amp[w, source] = jnp.concatenate(parts, axis=0).astype(half)
    vback[:, :, BLK:] = jnp.zeros((NW, 128 * BCH, 128 - BLK), half)
    contrib[:, :, 880:PACK] = jnp.zeros((YS, BLK, PACK - 880), single)
    def ycopy(k):
        ty, target = at_y(k)
        return pltpu.make_async_remote_copy(
            src_ref=contrib.at[ty], dst_ref=rbuf.at[k - 1],
            send_sem=rs_sem.at[k - 1], recv_sem=rr_sem.at[k - 1],
            device_id=target, device_id_type=MESH)

    gamma_row = square[pl.ds(irrep, 1), :]
    gamma_row = jnp.where(lax.broadcasted_iota(jnp.int32, (1, 128), 1) < BLK, gamma_row, 20.0)

    def source_step(index, _):
        source = lax.rem(y + index + 1, YS)

        place = lax.rem(index, 3)

        @pl.when(index == YS - 1)
        def _():
            def hole_step(p, _):
                hole_unit(YS - 1, p, 0)
                return 0

            lax.fori_loop(0, PER, hole_step, 0)

        for w in range(NW):
            for p in range(PER):
                here = pl.ds(source * PER + p, 1)
                alpha, energy = alphas[w, here, :], column_ref[0]
                for h in range(1, 8):
                    energy = jnp.where(alpha == h, column_ref[h], energy)
                column[BLK * p:BLK * p + BLK, :] = energy - bases[w, here, :]

            def lanes_of(t):
                return pl.ds(pl.multiple_of(t * 256, 256), 256)

            def particle(t):
                return jnp.dot(amp[w, source, :, :BLK], vt[w, :, lanes_of(t)], preferred_element_type=single)

            def stage(t, now, later, fill, drain):
                if later is not None:
                    later[...] = particle(t + 1)
                acc[...] += jnp.dot(
                    drain[...], vback[w, lanes_of(jnp.maximum(t - 1, 0)), :], preferred_element_type=single)
                for side in range(2):
                    b = 2 * t + side
                    rows = pl.ds(pl.multiple_of(b * BLK, 8), BLK)
                    hole = jnp.concatenate([
                        holes[place, rows, 256 * p + 128 * w:256 * p + 128 * w + 128] for p in range(PER)], axis=0)
                    energy = gamma_row + vir_ref[vtile, y * BCH + b]
                    inverse = pltpu.reciprocal(column[...] + energy, approx=True)
                    fill[:, 128 * side:128 * side + 128] = (
                        (now[:, 128 * side:128 * side + 128] - hole) * inverse).astype(half)

            acc[...] = jnp.zeros_like(acc)
            trip1[...] = jnp.zeros_like(trip1)
            part0[...] = particle(0)

            def two_steps(u, _):
                stage(2 * u, part0, part1, trip0, trip1)
                stage(2 * u + 1, part1, part0, trip1, trip0)
                return 0

            lax.fori_loop(0, BCH // 4, two_steps, 0)
            stage(BCH // 2 - 1, part0, None, trip0, trip1)
            acc[...] += jnp.dot(trip0[...], vback[w, 128 * (BCH - 2):, :], preferred_element_type=single)
            for p in range(PER):
                offset = BLK * (w * PER + p)
                contrib[source, :, offset:offset + BLK] = acc[BLK * p:BLK * p + BLK, :BLK]

        @pl.when(index < YS - 1)
        def _():
            ty, target = at_y(index + 1)
            pltpu.make_async_remote_copy(
                src_ref=contrib.at[ty], dst_ref=rbuf.at[index],
                send_sem=rs_sem.at[index], recv_sem=rr_sem.at[index],
                device_id=target, device_id_type=MESH).start()

        return 0

    lax.fori_loop(0, YS, source_step, 0)
    for k in (1, 2, 3):
        ycopy(k).wait()
    summed = contrib[y] + rbuf[0] + rbuf[1] + rbuf[2]
    windows = [summed[:, :OUTL], pltpu.roll(summed, PACK - 440, 1)[:, :OUTL]]
    lane = lax.broadcasted_iota(jnp.int32, (1, OUTL), 1)
    codes = []
    for w in range(NW):
        code = jnp.full((1, OUTL), -1, jnp.int32)
        for p in range(PER):
            inside = jnp.logical_and(lane >= BLK * p, lane < BLK * (p + 1))
            alpha = jnp.concatenate([alphas[w, pl.ds(y * PER + p, 1), :]] * 4, axis=1)
            code = jnp.where(inside, alpha, code)
        codes.append(code)
    ccopies, xcopies, zcopies = [], [], []
    for part in range(2):
        lanes = slice(256 * part, 256 * part + 256)
        for target in range(2 * XS):
            slots[part, target % 2, target // 2] = sum(
                jnp.where(codes[w][:, lanes] == target, windows[w][:, lanes], 0.0) for w in range(NW))
        ccopies.append(pltpu.make_async_remote_copy(
            src_ref=slots.at[part, 1 - core], dst_ref=cbuf.at[part],
            send_sem=cs_sem.at[part], recv_sem=cr_sem.at[part], device_id=at_core, device_id_type=MESH))
        ccopies[part].start()
    for part in range(2):
        ccopies[part].wait()
        for tx in range(XS):
            merged[part, tx] = slots[part, core, tx] + cbuf[part, tx]
        sends = []
        for k in (1, 3, 2):
            tx, target = at_x(k)
            sends.append(pltpu.make_async_remote_copy(
                src_ref=merged.at[part, tx], dst_ref=xbuf.at[part, k - 1],
                send_sem=xs_sem.at[part, k - 1], recv_sem=xr_sem.at[part, k - 1],
                device_id=target, device_id_type=MESH))
        for copy in sends:
            copy.start()
        xcopies.append(sends)
    for part in range(2):
        for copy in xcopies[part]:
            copy.wait()
        total[part] = merged[part, x] + xbuf[part, 0] + xbuf[part, 1] + xbuf[part, 2]
        zcopies.append(pltpu.make_async_remote_copy(
            src_ref=total.at[part, pl.ds(pl.multiple_of(40 * (1 - irrep), 8), 48), :], dst_ref=zbuf.at[part],
            send_sem=ts_sem.at[part], recv_sem=tr_sem.at[part], device_id=at_irrep, device_id_type=MESH))
        zcopies[part].start()
    def sent(n, _):
        @pl.when(z < ZS - 1)
        def _():
            chain_copy(True, n).wait_send()

        @pl.when(z > 0)
        def _():
            chain_copy(False, n).wait_send()

        return 0

    lax.fori_loop(0, TILES, sent, 0)

    def sent_y(n, _):
        for k in (1, 2, 3):
            slab_copy(k, n).wait_send()
        return 0

    lax.fori_loop(0, YN, sent_y, 0)
    for k in (1, 2, 3):
        hole_copy(k).wait_send()
        part_copy(k).wait_send()
    for index in range(RIGHT + LEFT):
        ring_copy(index).wait_send()
    for part in range(2):
        zcopies[part].wait()
        out_ref[:, 256 * part:256 * part + 256] = (
            total[part, pl.ds(pl.multiple_of(40 * irrep, 8), 48), :] + zbuf[part])


DMA = pltpu.SemaphoreType.DMA


def call(*operands):
    half, single = jnp.bfloat16, jnp.float32
    return pl.pallas_call(
        kernel,
        out_shape=jax.ShapeDtypeStruct((48, OUTL), single),
        in_specs=[SM] * 5 + [VM] * 5,
        out_specs=VM,
        scratch_shapes=[
            pltpu.VMEM((ALL, BLK, 128), half),
            pltpu.VMEM((YS, TILES, BLK, 128), half),
            pltpu.VMEM((TILES, NW, BLK, 128), half),
            pltpu.VMEM((TILES, NW, BLK, 128), half),
            pltpu.VMEM((TILES, NW, BLK, 128), half),
            pltpu.VMEM((TILES, NW, BLK, 128), half),
            pltpu.VMEM((YS, BLK, PACK), half),
            pltpu.VMEM((ZS, YS, 80, 128), half),
            pltpu.VMEM((YS * 80, 128), single),
            pltpu.VMEM((NW, 24 * 32, 128), single),
            pltpu.VMEM((NW, YS * PER, 128), jnp.int32),
            pltpu.VMEM((NW, YS * PER, 128), single),
            pltpu.VMEM((8, BLK, 128), single),
            pltpu.VMEM((128, 128), single),
            pltpu.VMEM((8, 128), single),
            pltpu.VMEM((2560, 128), single),
            pltpu.VMEM((CHL, 160), half),
            pltpu.VMEM((BLK, CHL), single),
            pltpu.VMEM((NW, BLK, 128 * BCH), half),
            pltpu.VMEM((NW, 128 * BCH, 128), half),
            pltpu.VMEM((NW, YS, PER * BLK, 128), half),
            pltpu.VMEM((YS, 160, 256 * PER), half),
            pltpu.VMEM((3, BCH * BLK, 256 * PER), single),
            pltpu.VMEM((PER * BLK, 128), single),
            pltpu.VMEM((PER * BLK, 128), single),
            pltpu.VMEM((PER * BLK, 256), single),
            pltpu.VMEM((PER * BLK, 256), single),
            pltpu.VMEM((PER * BLK, 256), half),
            pltpu.VMEM((PER * BLK, 256), half),
            pltpu.VMEM((YS, BLK, PACK), single),
            pltpu.VMEM((3, BLK, PACK), single),
            pltpu.VMEM((2, 2, XS, BLK, 256), single),
            pltpu.VMEM((2, XS, BLK, 256), single),
            pltpu.VMEM((2, XS, BLK, 256), single),
            pltpu.VMEM((2, 3, BLK, 256), single),
            pltpu.VMEM((2, BLK, 256), single),
            pltpu.VMEM((2, 48, 256), single),
            DMA((3, YN)), DMA((3, YN)), DMA((3,)), DMA((3,)), DMA((3,)), DMA((3,)),
            DMA((TILES,)), DMA((TILES,)), DMA((TILES,)), DMA((TILES,)), DMA((7,)), DMA((7,)), DMA((3,)),
            DMA((3,)), DMA((3,)), DMA((2,)), DMA((2,)), DMA((2, 3)), DMA((2, 3)), DMA((2,)), DMA((2,)),
        ],
        compiler_params=pltpu.CompilerParams(
            collective_id=0, has_side_effects=True, vmem_limit_bytes=62 * 2**20),
    )(*operands)


def pick(table, index):
    places = jnp.arange(table.shape[0], dtype=jnp.int32)
    return jnp.sum(jnp.where(index[..., None] == places, table, 0), axis=-1)


def on_device(
    amplitudes, slabs, couplings, occ_energy, vir_energy, occ_irrep, pair_i, pair_j, window_k, owner
):
    half = jnp.bfloat16
    pair, beta, gamma, y, z = where_am_i()
    k_irrep = pick(occ_irrep, window_k)
    pair_sym = pick(occ_irrep, pair_i) ^ pick(occ_irrep, pair_j)
    alpha = pair_sym[None, :] ^ k_irrep[:, None] ^ beta ^ gamma
    index = jnp.concatenate([(beta ^ pair_sym)[:, None], alpha.T], axis=1)
    blocks = jnp.take_along_axis(amplitudes, index[:, :, None], axis=1).reshape(PER, 1 + NW, BLK, BLK)
    send = blocks[:, 0].swapaxes(1, 2).reshape(PER, YS, BCH * BLK)
    tags = jnp.stack([pair_i, pair_j], axis=1).astype(half)[:, None, :]
    tail = jnp.pad(jnp.broadcast_to(tags, (PER, YS, 2)), ((0, 0), (0, 0), (0, CHL - BCH * BLK - 2)))
    hole = jnp.concatenate([send, tail], axis=2).swapaxes(0, 1).reshape(YS, PER * 16, 128)
    part = blocks[:, 1:].transpose(2, 1, 0, 3).reshape(BLK, NW * PER * BLK)
    part = jnp.pad(part, ((0, 0), (0, PACK - NW * PER * BLK)))

    result = call(
        owner, occ_irrep, occ_energy, window_k, vir_energy,
        slabs.reshape(BLK, BLK * BLK), part, hole, couplings, vir_energy)
    result = lax.dynamic_slice_in_dim(result, 4 * gamma, BLK // 2, 0)[:, :PER * BLK]
    return result.reshape(BLK // 2, PER, BLK).swapaxes(0, 1).reshape(PER, 1, BLK * BLK // 2)


def solution(mesh):
    placed = (
        P("pair", None, None),
        P("pair", "vtile", "irrep", None, None),
        P(None, None, None, "irrep"),
        P(),
        P(),
        P(),
        P("pair"),
        P("pair"),
        P(),
        P(),
    )
    return jax.shard_map(
        on_device,
        mesh=mesh,
        in_specs=placed,
        out_specs=P("pair", "vtile", "irrep"),
        check_vma=False,
    )
```
